32 devices in a mesh: groups: 2 (over y), rep: 4 (over x, core), tp: 4 (over z).
Axes of the slice: x: 2, y: 2, z: 4, core: 2. Of those that a mesh axis runs over, the one named last changes fastest.
Arguments:
- features: bfloat16 [4096, 8192], P(('groups', 'rep'), 'tp'), parts along dimension 0, may hold values from -6 to 6
- query_weight: bfloat16 [8192, 8192], P(None, 'tp'), may hold values from -0.0625 to 0.0625
- adapter_down: bfloat16 [128, 16, 8192], P('rep', None, 'tp'), may hold values from -0.0625 to 0.0625
- adapter_up: bfloat16 [128, 16, 8192], P('rep', None, 'tp'), may hold values from -1.5 to 1.5
- block_owner: int32 [128, 1], P(('groups', 'rep')), parts along dimension 0, may hold values from 0 to 3; in each aligned block of 16 rows (0 to 15, 16 to 31, ...) at most 8 rows name the same one
- block_slot: int32 [128], P(('groups', 'rep')), parts along dimension 0, may hold values from 0 to 31
Outputs:
- queries: bfloat16 [4096, 8192], P(('groups', 'rep'), 'tp'), parts along dimension 0
The draws below stay inside these ranges and needn't reach their ends.
There are 2 independent parts, one for each index of `groups`. The reference program is written for one: setup_inputs(seed, part) draws one part's arguments, and reference() takes and returns one part's arrays. A program takes and returns all parts, laid end to end along the dimension named above; an argument that names none is the same for every part. Nothing has to cross between parts.
Inputs may be any that keep to these rules, and one draw needn't show every extreme that they name: `block_owner`: among the 16 batches of one index of rep, no owner is named more than 8 times, a bound that some block reaches.
All inputs are finite; a program needn't handle non-finite values.
Results may differ from the reference program's by a relative error of at most 0.004.
Values may be sent and summed in bfloat16 or wider, within the bound.
No kernel may reach another device: no remote copies, remote signals or barrier semaphores. Data moves between devices by JAX's collectives and lax.ppermute only.
A program may use at most 192 MiB of HBM per device.

```python
import math
import jax
import jax.numpy as jnp
import numpy as np

D = 8192
QOUT = 8192
RANK = 16
TOKS = 2
BLOCK = 16
ADP_DEV = 32
NB_DEV = 16
CAP = 8
NADAPT = 128
NBLK = 64
ROWS = 2048
N_REP = 4


def plant(values, key, smallest, top_value):
    longest = values.shape.index(max(values.shape))
    spots = []
    for shift in (0, 1):
        where = [jax.random.randint(jax.random.fold_in(key, axis), (), 0, length) for axis, length in enumerate(values.shape)]
        where[longest] = (where[longest] + shift) % values.shape[longest]
        spots.append(tuple(where))
    return values.at[spots[0]].set(smallest).at[spots[1]].set(top_value)


def level_of(stream_key, shape, pieces, low, largest):
    def one(dim, parts):
        heights = jax.random.uniform(jax.random.fold_in(jax.random.fold_in(stream_key, 6), dim), (parts,), jnp.float32, low / len(pieces), largest / len(pieces))
        return jnp.repeat(jnp.exp(heights), shape[dim] // parts).reshape((-1,) + (1,) * (len(shape) - dim - 1))

    gain = one(*pieces[0])
    for cut in pieces[1:]:
        gain = gain * one(*cut)
    return gain


def deal_out(own_key, own, number, rows, amount, top, bound, slope):
    order = jax.random.permutation(own_key, amount)
    crowded, common = load_shares(amount, rows * top, bound, slope, True), load_shares(amount, rows * top, bound, slope, False)
    places = jnp.arange(amount)

    def named(sizes, turn):
        used = int((sizes > 0).sum())
        fixed = max(1, used // 4)
        moved = fixed + (places - fixed + turn * (used - fixed)) % max(1, amount - fixed)
        return jnp.zeros((amount,), jnp.int32).at[order[jnp.where(places < fixed, places, moved)]].set(jnp.asarray(sizes, jnp.int32))

    sizes = jnp.where(number % 4 == 0, named(crowded, number // 4), named(common, number - number // 4 - 1))
    mixed = jax.random.permutation(jax.random.fold_in(own, 3), amount)
    donor, sink = mixed[0:amount // 2 * 2:2], mixed[1:amount // 2 * 2:2]
    margin = jnp.minimum(sizes[donor] - 1, bound - sizes[sink]) // 2
    margin = jnp.where((donor == order[0]) | (sink == order[0]) | (sizes[sink] == 0), 0, jnp.maximum(margin, 0))
    moved = jax.random.randint(jax.random.fold_in(own, 4), (amount // 2,), 0, 1 << 20) % (margin + 1)
    sizes = sizes.at[donor].add(-moved).at[sink].add(moved)
    items = jnp.searchsorted(jnp.cumsum(sizes), jnp.arange(rows * top), side="right").astype(jnp.int32)
    listing = items.reshape(top, rows).T
    listing = listing[jax.random.permutation(jax.random.fold_in(own, 1), rows)]
    turn = jax.random.randint(jax.random.fold_in(own, 2), (rows, 1), 0, top)
    return jnp.take_along_axis(listing, (jnp.arange(top)[None, :] + turn) % top, axis=1)


def load_shares(amount, total, bound, skew, full):
    weights = [(1 << 20) // math.isqrt(standing ** skew) + 1 for standing in range(1, amount + 1)]
    largest = bound if full else min(bound, max(-(-total // amount), total * weights[0] // sum(weights)))
    least = 1 if total - largest >= amount - 1 else 0
    counts, surplus = [largest] + [least] * (amount - 1), total - largest - least * (amount - 1)
    while surplus > 0:
        candidates = [i for i in range(1, amount) if counts[i] < largest] or [i for i in range(1, amount) if counts[i] < bound]
        pool, budget = sum([weights[i] for i in candidates]), surplus
        for i in candidates:
            more = min(bound - counts[i], max(1, budget * weights[i] // pool), surplus)
            counts[i] = counts[i] + more
            surplus = surplus - more
    return np.array(counts)


def scatter_about(key, dims, width, bound, pieces=(), held_as=jnp.bfloat16):
    drawn = width * jax.random.normal(key, dims, jnp.float32)
    if pieces:
        drawn = drawn * level_of(key, dims, pieces, -0.22, 0.18)
    return jnp.clip(drawn, -bound, bound).astype(held_as)


def setup_inputs(seed: int = 0, part: int = 0) -> dict:
    keys = jax.random.split(jax.random.key(seed), 7)
    part_keys = jax.random.split(jax.random.fold_in(keys[6], part), 7)
    features = scatter_about(part_keys[0], (ROWS, D), 1.0, 6.0, ((0, 4), (1, 4)))
    query_weight = scatter_about(keys[1], (D, QOUT), D ** -0.5, 0.0625, ((1, 4),))
    adapter_down = scatter_about(keys[2], (NADAPT, RANK, D), D ** -0.5, 0.0625, ((0, 4), (2, 4)))
    adapter_up = scatter_about(keys[3], (NADAPT, RANK, QOUT), RANK ** -0.5, 1.5, ((0, 4), (2, 4)))
    block_owner_keys = jax.random.split(jax.random.fold_in(part_keys[4], 1), NBLK // NB_DEV)
    block_owner_turns = jax.random.permutation(jax.random.fold_in(part_keys[4], 3), NBLK // NB_DEV)
    block_owner = jax.vmap(lambda own, number: deal_out(jax.random.fold_in(part_keys[4], 2), own, number, NB_DEV, N_REP, 1, CAP, 2))(block_owner_keys, block_owner_turns).reshape((NBLK, 1))
    block_slot = plant(jax.random.randint(part_keys[5], (NBLK,), 0, ADP_DEV), jax.random.fold_in(part_keys[5], 1), 0, ADP_DEV - 1).astype(jnp.int32)
    return dict(features=features, query_weight=query_weight, adapter_down=adapter_down, adapter_up=adapter_up, block_owner=block_owner, block_slot=block_slot)


def reference(features, query_weight, adapter_down, adapter_up, block_owner, block_slot):
    adapter = (block_owner[:, 0] * ADP_DEV + block_slot).astype(jnp.int32)
    projected = jnp.dot(features, query_weight, preferred_element_type=jnp.float32)
    selected_down_weight = jnp.take(adapter_down, adapter, axis=0).astype(jnp.float32)
    chosen_up = jnp.take(adapter_up, adapter, axis=0).astype(jnp.float32)
    rows_by_adapter = features.reshape(NBLK, BLOCK * TOKS, D).astype(jnp.float32)
    down_projected = jnp.einsum("qlo,qfo->qlf", rows_by_adapter, selected_down_weight).astype(jnp.bfloat16)
    adapter_term = jnp.einsum("brk,bko->bro", down_projected.astype(jnp.float32), chosen_up)
    total = projected.reshape(NBLK, BLOCK * TOKS, QOUT) + adapter_term
    return total.reshape(ROWS, QOUT).astype(jnp.bfloat16)
```

```python
import functools

import jax
import jax.numpy as jnp
from jax import lax
from jax.experimental import pallas as pl
from jax.experimental.pallas import tpu as pltpu
from jax.sharding import PartitionSpec as P

F32 = jnp.float32
BF16 = jnp.bfloat16
PIECES = 2
ANY = pl.BlockSpec(memory_space=pl.ANY)
VMEM = pl.BlockSpec(memory_space=pltpu.VMEM)


def params(mib):
    return pltpu.CompilerParams(vmem_limit_bytes=mib << 20)


def dot(x, w):
    return jnp.dot(x, w, preferred_element_type=F32)


def wanted(block_owner, block_slot, rep):
    owners = block_owner[:, 0]
    blocks = owners.shape[0]
    cap = 2 * blocks // rep
    order = jnp.arange(blocks)
    earlier = (owners[None, :] == owners[:, None]) & (order[None, :] < order[:, None])
    rank = jnp.sum(earlier, axis=1, dtype=jnp.int32)
    source = jnp.bitwise_xor(owners, lax.axis_index("rep"))
    landing = source * cap + rank
    asked = jnp.sum(
        jnp.where(landing[None, :] == jnp.arange(rep * cap)[:, None], block_slot[None, :], 0), axis=1, dtype=jnp.int32
    ).reshape(rep, cap)
    lists = [lax.ppermute(asked[i], "rep", [(r, r ^ i) for r in range(rep)]) for i in range(1, rep)]
    return lists, source, jnp.where(source == 0, block_slot, rank)


def pack_kernel(count, cap, *refs):
    lists, (down, up), outs, sems = refs[:count], refs[count : count + 2], refs[count + 2 : -1], refs[-1]
    copies = []
    for i in range(count):
        for j in range(cap):
            slot = lists[i][j]
            for k, pool in enumerate((down, up)):
                at = k * cap + j
                copies.append(pltpu.make_async_copy(pool.at[slot], outs[i].at[at], sems.at[i, at]))
    for copy in copies:
        copy.start()
    for copy in copies:
        copy.wait()


def pack(lists, down, up):
    count, cap = len(lists), lists[0].shape[0]
    shape = jax.ShapeDtypeStruct((2 * cap,) + down.shape[1:], down.dtype)
    moved = count * 2 * cap * down.shape[1] * down.shape[2] * 4
    return pl.pallas_call(
        functools.partial(pack_kernel, count, cap),
        out_shape=[shape] * count,
        in_specs=[pl.BlockSpec(memory_space=pltpu.SMEM)] * count + [ANY] * 2,
        out_specs=[ANY] * count,
        scratch_shapes=[pltpu.SemaphoreType.DMA((count, 2 * cap))],
        cost_estimate=pl.CostEstimate(flops=0, bytes_accessed=moved, transcendentals=0),
        compiler_params=params(8),
        name="pack_blocks",
    )(*lists, down, up)


def shrink_kernel(rep, cap, source, place, features, down, up, *refs):
    held, (part, chosen_up), (chosen_down, sems) = refs[: rep - 1], refs[rep - 1 : rep + 1], refs[rep + 1 :]
    blocks = source.shape[0]
    rank = down.shape[1]

    def pair(b, i):
        at = place[b]
        one = down.at[at] if i == 0 else held[i - 1].at[at]
        two = up.at[at] if i == 0 else held[i - 1].at[cap + at]
        return (
            pltpu.make_async_copy(one, chosen_down.at[pl.ds(b * rank, rank)], sems.at[0, b]),
            pltpu.make_async_copy(two, chosen_up.at[pl.ds(b * rank, rank)], sems.at[1, b]),
        )

    for b in range(blocks):
        for i in range(rep):

            @pl.when(source[b] == i)
            def _():
                for copy in pair(b, i):
                    copy.start()

    for b in range(blocks):
        for i in range(rep):

            @pl.when(source[b] == i)
            def _():
                for copy in pair(b, i):
                    copy.wait()

    rows = features.shape[0]
    every = lax.dot_general(
        chosen_down[...], features[...], (((1,), (1,)), ((), ())), preferred_element_type=F32
    ).reshape(blocks, rank, rows)
    batch = lax.broadcasted_iota(jnp.int32, every.shape, 2) // (rows // blocks)
    own = batch == lax.broadcasted_iota(jnp.int32, every.shape, 0)
    part[...] = jnp.sum(jnp.where(own, every, 0.0), axis=0)


def shrink(source, place, features, down, up, held):
    blocks, rows = source.shape[0], features.shape[0]
    _, rank, depth = down.shape
    rep = len(held) + 1
    cap = held[0].shape[0] // 2
    return pl.pallas_call(
        functools.partial(shrink_kernel, rep, cap),
        out_shape=[
            jax.ShapeDtypeStruct((rank, rows), F32),
            jax.ShapeDtypeStruct((blocks * rank, depth), BF16),
        ],
        in_specs=[pl.BlockSpec(memory_space=pltpu.SMEM)] * 2 + [VMEM] + [ANY] * (2 + len(held)),
        out_specs=[VMEM, ANY],
        scratch_shapes=[pltpu.VMEM((blocks * rank, depth), BF16), pltpu.SemaphoreType.DMA((2, blocks))],
        cost_estimate=pl.CostEstimate(flops=2 * blocks * rank * rows * depth, bytes_accessed=rows * depth * 2, transcendentals=0),
        compiler_params=params(16),
        name="shrink",
    )(source, place, features, down, up, *held)


def spread(total, blocks):
    rank, rows = total.shape
    tall = jnp.concatenate([total] * blocks, axis=0)
    batch = lax.broadcasted_iota(jnp.int32, tall.shape, 1) // (rows // blocks)
    own = batch == lax.broadcasted_iota(jnp.int32, tall.shape, 0) // rank
    return jnp.where(own, tall, 0.0).astype(BF16)


def add_kernel(pieces, choices, tail, *refs):
    info = refs[0]
    cands = refs[1 : 1 + pieces * choices]
    rest = list(refs[1 + pieces * choices :])
    weight = rest.pop(0)
    acc = rest.pop(0) if tail["acc"] else None
    sums = [rest.pop(0) for _ in range(tail["sums"])]
    up = rest.pop(0) if tail["sums"] else None
    if tail["kept"]:
        rest.pop(0)
    out, x, sems = rest[0], rest[1], rest[2]
    wide = rest[3] if tail["sums"] else None
    step = x.shape[0] // pieces

    def copy(c, i):
        return pltpu.make_async_copy(cands[c * choices + i], x.at[pl.ds(c * step, step)], sems.at[c])

    @pl.when(pl.program_id(0) == 0)
    def _():
        for c in range(pieces):
            for i in range(choices):

                @pl.when(info[0] == i)
                def _():
                    copy(c, i).start()

        if tail["sums"]:
            total = sums[0][...]
            for more in sums[1:]:
                total = total + more[...]
            wide[...] = spread(total, tail["blocks"])
        for c in range(pieces):
            for i in range(choices):

                @pl.when(info[0] == i)
                def _():
                    copy(c, i).wait()

    total = dot(x[...], weight[...])
    if acc is not None:
        total = total + acc[...]
    if tail["sums"]:
        total = total + lax.dot_general(wide[...], up[...], (((0,), (0,)), ((), ())), preferred_element_type=F32)
    out[...] = total.astype(out.dtype)


def add_part(cands, which, part, weight, acc=None, sums=(), up=None, blocks=0, final=None, tile=512):
    pieces, choices = len(cands), len(cands[0])
    step, depth = cands[0][0].shape
    rows, cols = pieces * step, weight.shape[1]
    at = final[0] if final else 0
    out_rows = acc.shape[0] if final else rows
    tail = {"acc": acc is not None, "sums": len(sums), "blocks": blocks, "kept": bool(final and final[1] is not None)}
    args = [jnp.stack([which, part]).astype(jnp.int32)] + [x for piece in cands for x in piece] + [weight]
    specs = [ANY] * (pieces * choices) + [pl.BlockSpec((depth, tile), lambda j, info: (info[1], j))]
    block = pl.BlockSpec((rows, tile), lambda j, info: (at, j))
    aliases = {}
    if acc is not None:
        if not final:
            aliases[len(args)] = 0
        args.append(acc)
        specs.append(block)
    for s in sums:
        args.append(s)
        specs.append(pl.BlockSpec(s.shape, lambda j, info: (0, 0)))
    scratch = [pltpu.VMEM((rows, depth), BF16), pltpu.SemaphoreType.DMA((pieces,))]
    if sums:
        args.append(up)
        specs.append(pl.BlockSpec((up.shape[0], tile), lambda j, info: (0, j)))
        scratch.append(pltpu.VMEM((up.shape[0], rows), BF16))
    if tail["kept"]:
        aliases[len(args)] = 0
        args.append(final[1])
        specs.append(ANY)
    return pl.pallas_call(
        functools.partial(add_kernel, pieces, choices, tail),
        out_shape=jax.ShapeDtypeStruct((out_rows, cols), BF16 if final else F32),
        grid_spec=pltpu.PrefetchScalarGridSpec(
            num_scalar_prefetch=1, grid=(cols // tile,), in_specs=specs, out_specs=block, scratch_shapes=scratch
        ),
        input_output_aliases=aliases,
        cost_estimate=pl.CostEstimate(
            flops=2 * rows * depth * cols, bytes_accessed=2 * depth * cols + 8 * rows * cols, transcendentals=0
        ),
        compiler_params=params(32),
        name="add_part",
    )(*args)


def line_of_four(features, query_weight, part_of_shrink, blocks):
    z = lax.axis_index("tp")
    pick = lambda values: jnp.array(values, jnp.int32)[z]
    pieces = jnp.split(features, PIECES)
    right, left = [(0, 1), (1, 2), (2, 3)], [(1, 0), (2, 1), (3, 2)]
    r1, l1, r2, l2, far = [], [], [], [], []
    for p in pieces:
        r1.append(lax.ppermute(p, "tp", right))
        l1.append(lax.ppermute(p, "tp", left))
    for c in range(PIECES):
        r2.append(lax.ppermute(r1[c], "tp", right[1:]))
        l2.append(lax.ppermute(l1[c], "tp", left[:-1]))
    for c in range(PIECES):
        far.append(lax.ppermute(jnp.where(z == 1, l2[c], r2[c]), "tp", [(1, 0), (2, 3)]))
    acc = add_part([[features]], z * 0, z, query_weight)
    acc = add_part(list(zip(l1, r1)), pick([0, 1, 1, 1]), pick([1, 0, 1, 2]), query_weight, acc)
    mine, up = part_of_shrink
    sums = [mine] + [lax.ppermute(mine, "tp", [(i, (i + d) % 4) for i in range(4)]) for d in (1, 2, 3)]
    acc = add_part(
        list(zip(l1, r2, l2)), pick([2, 0, 0, 1]), pick([2, 2, 3, 1]), query_weight, acc, sums, up, blocks
    )
    out = None
    for c in range(PIECES):
        out = add_part(
            [[l2[c], r2[c], far[c]]], pick([2, 0, 1, 2]), pick([3, 3, 0, 0]), query_weight, acc, final=(c, out)
        )
    return out


def solution(mesh):
    tp, rep = mesh.shape["tp"], mesh.shape["rep"]

    def on_device(features, query_weight, adapter_down, adapter_up, block_owner, block_slot):
        lists, source, place = wanted(block_owner, block_slot, rep)
        packed = pack(lists, adapter_down, adapter_up)
        held = [lax.ppermute(p, "rep", [(r, r ^ (i + 1)) for r in range(rep)]) for i, p in enumerate(packed)]
        mine, up = shrink(source, place, features, adapter_down, adapter_up, held)
        blocks = block_slot.shape[0]
        if tp == 4:
            return line_of_four(features, query_weight, (mine, up), blocks)
        base = dot(lax.all_gather(features, "tp", axis=1, tiled=True), query_weight)
        extra = dot(spread(lax.psum(mine, "tp"), blocks).T, up)
        return (base + extra).astype(BF16)

    placed = (
        P(("groups", "rep"), "tp"),
        P(None, "tp"),
        P("rep", None, "tp"),
        P("rep", None, "tp"),
        P(("groups", "rep"), None),
        P(("groups", "rep")),
    )
    return jax.shard_map(
        on_device, mesh=mesh, in_specs=placed, out_specs=P(("groups", "rep"), "tp"), check_vma=False
    )
```

```python
import functools

import jax
import jax.numpy as jnp
from jax import lax
from jax.experimental import pallas as pl
from jax.experimental.pallas import tpu as pltpu
from jax.sharding import PartitionSpec as P

F32 = jnp.float32
BF16 = jnp.bfloat16
PIECE = (3, 4)
ANY = pl.BlockSpec(memory_space=pl.ANY)
VMEM = pl.BlockSpec(memory_space=pltpu.VMEM)


def params(mib):
    return pltpu.CompilerParams(vmem_limit_bytes=mib << 20)


def dot(x, w):
    return jnp.dot(x, w, preferred_element_type=F32)


def wanted(block_owner, block_slot, rep):
    owners = block_owner[:, 0]
    blocks = owners.shape[0]
    cap = 2 * blocks // rep
    order = jnp.arange(blocks)
    earlier = (owners[None, :] == owners[:, None]) & (order[None, :] < order[:, None])
    rank = jnp.sum(earlier, axis=1, dtype=jnp.int32)
    source = jnp.bitwise_xor(owners, lax.axis_index("rep"))
    landing = source * cap + rank
    asked = jnp.sum(
        jnp.where(landing[None, :] == jnp.arange(rep * cap)[:, None], block_slot[None, :], 0), axis=1, dtype=jnp.int32
    ).reshape(rep, cap)
    return asked, source, jnp.where(source == 0, block_slot, rank)


def swap(x, distance, rep):
    return lax.ppermute(x, "rep", [(r, r ^ distance) for r in range(rep)])


def after(x, *earlier):
    return lax.optimization_barrier((x,) + earlier)[0]


def in_turn(parts, rep):
    got = []
    for i, part in enumerate(parts):
        got.append(swap(after(part, *got[-1:]), i + 1, rep))
    return got


def pack_kernel(count, cap, *refs):
    lists, pool, outs, sems = refs[:count], refs[count], refs[count + 1 : -1], refs[-1]
    copies = []
    for i in range(count):
        for j in range(cap):
            copies.append(pltpu.make_async_copy(pool.at[lists[i][j]], outs[i].at[j], sems.at[i, j]))
    for copy in copies:
        copy.start()
    for copy in copies:
        copy.wait()


def pack(lists, pool):
    count, cap = len(lists), lists[0].shape[0]
    shape = jax.ShapeDtypeStruct((cap,) + pool.shape[1:], pool.dtype)
    moved = count * cap * pool.shape[1] * pool.shape[2] * 4
    return pl.pallas_call(
        functools.partial(pack_kernel, count, cap),
        out_shape=[shape] * count,
        in_specs=[pl.BlockSpec(memory_space=pltpu.SMEM)] * count + [ANY],
        out_specs=[ANY] * count,
        scratch_shapes=[pltpu.SemaphoreType.DMA((count, cap))],
        cost_estimate=pl.CostEstimate(flops=0, bytes_accessed=moved, transcendentals=0),
        compiler_params=params(8),
        name="pack_blocks",
    )(*lists, pool)


def choose(source, place, pool, held, chosen, sems):
    blocks, rank = source.shape[0], pool.shape[1]

    def each(act):
        for b in range(blocks):
            for i in range(len(held) + 1):

                @pl.when(source[b] == i)
                def _():
                    block = (pool if i == 0 else held[i - 1]).at[place[b]]
                    act(pltpu.make_async_copy(block, chosen.at[pl.ds(b * rank, rank)], sems.at[b]))

    each(lambda copy: copy.start())
    each(lambda copy: copy.wait())


def choose_kernel(source, place, pool, *refs):
    choose(source, place, pool, refs[:-2], refs[-2], refs[-1])


def chosen_blocks(source, place, pool, held):
    blocks = source.shape[0]
    _, rank, depth = pool.shape
    return pl.pallas_call(
        choose_kernel,
        out_shape=jax.ShapeDtypeStruct((blocks * rank, depth), pool.dtype),
        in_specs=[pl.BlockSpec(memory_space=pltpu.SMEM)] * 2 + [ANY] * (1 + len(held)),
        out_specs=ANY,
        scratch_shapes=[pltpu.SemaphoreType.DMA((blocks,))],
        cost_estimate=pl.CostEstimate(flops=0, bytes_accessed=blocks * rank * depth * 4, transcendentals=0),
        compiler_params=params(8),
        name="choose_blocks",
    )(source, place, pool, *held)


def shrink_kernel(source, place, features, pool, *refs):
    held, part, chosen, sems = refs[:-3], refs[-3], refs[-2], refs[-1]
    blocks, rank, rows = source.shape[0], pool.shape[1], features.shape[0]
    choose(source, place, pool, held, chosen, sems)
    every = lax.dot_general(
        chosen[...], features[...], (((1,), (1,)), ((), ())), preferred_element_type=F32
    ).reshape(blocks, rank, rows)
    batch = lax.broadcasted_iota(jnp.int32, every.shape, 2) // (rows // blocks)
    own = batch == lax.broadcasted_iota(jnp.int32, every.shape, 0)
    part[...] = jnp.sum(jnp.where(own, every, 0.0), axis=0)


def shrink(source, place, features, down, held):
    blocks, rows = source.shape[0], features.shape[0]
    _, rank, depth = down.shape
    return pl.pallas_call(
        shrink_kernel,
        out_shape=jax.ShapeDtypeStruct((rank, rows), F32),
        in_specs=[pl.BlockSpec(memory_space=pltpu.SMEM)] * 2 + [VMEM] + [ANY] * (1 + len(held)),
        out_specs=VMEM,
        scratch_shapes=[pltpu.VMEM((blocks * rank, depth), BF16), pltpu.SemaphoreType.DMA((blocks,))],
        cost_estimate=pl.CostEstimate(flops=2 * blocks * rank * rows * depth, bytes_accessed=rows * depth * 2, transcendentals=0),
        compiler_params=params(16),
        name="shrink",
    )(source, place, features, down, *held)


def spread(total, blocks):
    rank, rows = total.shape
    tall = jnp.concatenate([total] * blocks, axis=0)
    batch = lax.broadcasted_iota(jnp.int32, tall.shape, 1) // (rows // blocks)
    own = batch == lax.broadcasted_iota(jnp.int32, tall.shape, 0) // rank
    return jnp.where(own, tall, 0.0).astype(BF16)


def add_kernel(choices, tail, *refs):
    info, cands = refs[0], refs[1 : 1 + choices]
    rest = list(refs[1 + choices :])
    weight = rest.pop(0)
    acc = rest.pop(0) if tail["acc"] else None
    sums = [rest.pop(0) for _ in range(tail["sums"])]
    up = rest.pop(0) if sums else None
    if tail["kept"]:
        rest.pop(0)
    out, x, sem = rest[:3]
    wide = rest[3] if sums else None
    which = info[tail["which"]]

    def each(act):
        for i, cand in enumerate(cands):

            @pl.when(which == i)
            def _():
                rows = x.shape[0]
                first = 0 if cand.shape[0] == rows else tail["first"]
                act(pltpu.make_async_copy(cand.at[pl.ds(first, rows)], x, sem))

    @pl.when(pl.program_id(0) == 0)
    def _():
        each(lambda copy: copy.start())
        if sums:
            wide[...] = spread(sum(s[...] for s in sums), tail["blocks"])
        each(lambda copy: copy.wait())

    tile = out.shape[1]
    if weight.shape[1] == tile:
        total = dot(x[...], weight[...])
    else:
        total = dot(x[...], weight[:, pl.ds(pl.multiple_of(pl.program_id(0) * tile, tile), tile)])
    if acc is not None:
        total = total + acc[...]
    if sums:
        total = total + lax.dot_general(wide[...], up[...], (((0,), (0,)), ((), ())), preferred_element_type=F32)
    out[...] = total.astype(out.dtype)


def add_part(info, at, cands, weight, acc=None, sums=(), up=None, blocks=0, final=None, tile=512):
    whole, depth = cands[0].shape
    cols = weight.shape[1]
    first, end, kept = final if final else (0, whole, None)
    rows = end - first
    tail = {
        "acc": acc is not None,
        "blocks": blocks,
        "sums": len(sums),
        "kept": kept is not None,
        "which": at,
        "first": first,
    }
    args = [info, *cands, weight]
    specs = [ANY] * len(cands)
    if final:
        specs.append(VMEM)
    else:
        specs.append(pl.BlockSpec((depth, tile), lambda j, info: (info[at + 1], j)))
    block = pl.BlockSpec((rows, tile), lambda j, info: (first // rows, j))
    aliases = {}
    if acc is not None:
        if not final:
            aliases[len(args)] = 0
        args.append(acc)
        specs.append(block)
    scratch = [pltpu.VMEM((rows, depth), BF16), pltpu.SemaphoreType.DMA]
    if blocks:
        args += [*sums, up]
        specs += [pl.BlockSpec(s.shape, lambda j, info: (0, 0)) for s in sums]
        specs.append(pl.BlockSpec((up.shape[0], tile), lambda j, info: (0, j)))
        scratch.append(pltpu.VMEM((up.shape[0], rows), BF16))
    if kept is not None:
        aliases[len(args)] = 0
        args.append(kept)
        specs.append(ANY)
    return pl.pallas_call(
        functools.partial(add_kernel, len(cands), tail),
        out_shape=jax.ShapeDtypeStruct((whole, cols), BF16 if final else F32),
        grid_spec=pltpu.PrefetchScalarGridSpec(
            num_scalar_prefetch=1, grid=(cols // tile,), in_specs=specs, out_specs=block, scratch_shapes=scratch
        ),
        input_output_aliases=aliases,
        cost_estimate=pl.CostEstimate(
            flops=2 * rows * depth * cols, bytes_accessed=2 * depth * cols + 8 * rows * cols, transcendentals=0
        ),
        compiler_params=params(24),
        name="add_part",
    )(*args)


def fetch_kernel(at, info, weight, out, sem):
    depth = out.shape[0]
    copy = pltpu.make_async_copy(weight.at[pl.ds(pl.multiple_of(info[at] * depth, depth), depth)], out, sem)
    copy.start()
    copy.wait()


def fetch_part(info, at, weight, depth):
    return pl.pallas_call(
        functools.partial(fetch_kernel, at),
        out_shape=jax.ShapeDtypeStruct((depth, weight.shape[1]), weight.dtype),
        in_specs=[pl.BlockSpec(memory_space=pltpu.SMEM), ANY],
        out_specs=ANY,
        scratch_shapes=[pltpu.SemaphoreType.DMA],
        cost_estimate=pl.CostEstimate(flops=0, bytes_accessed=4 * depth * weight.shape[1], transcendentals=0),
        compiler_params=params(1),
        name="fetch_part",
    )(info, weight)


CHOICES = (
    (0, 0, 0, 1, 2, 2, 2, 3),
    (0, 1, 1, 0, 0, 2, 0, 3),
    (0, 2, 1, 1, 0, 3, 1, 0),
    (0, 3, 1, 2, 1, 1, 2, 0),
)


def on_line_of_four(features, query_weight, adapter_down, adapter_up, block_owner, block_slot, rep):
    z = lax.axis_index("tp")
    info = lax.dynamic_index_in_dim(jnp.array(CHOICES, jnp.int32), z, 0, keepdims=False)
    right, left = [(0, 1), (1, 2), (2, 3)], [(1, 0), (2, 1), (3, 2)]
    rows, blocks = features.shape[0], block_slot.shape[0]
    cut = rows * PIECE[0] // PIECE[1]

    asked, source, place = wanted(block_owner, block_slot, rep)
    r1, l1 = lax.ppermute(features, "tp", right), lax.ppermute(features, "tp", left)
    lists = in_turn(list(asked[1:]), rep)
    downs = in_turn(pack(lists, adapter_down), rep)
    acc = add_part(after(info, *lists), 0, [features], query_weight)
    packed = pack([after(lists[0], acc)] + lists[1:], adapter_up)
    r2, l2 = lax.ppermute(after(r1, acc, *downs), "tp", right[1:]), lax.ppermute(after(l1, acc, *downs), "tp", left[:-1])
    mine = shrink(after(source, acc, r1, l1), place, features, adapter_down, downs)
    acc = add_part(after(info, mine), 2, [l1, r1], query_weight, acc)
    ups = in_turn([after(packed[0], mine), *packed[1:]], rep)
    up = chosen_blocks(after(source, acc), place, adapter_up, ups)
    ready = after(mine, acc, up)
    shares = [mine] + [lax.ppermute(ready, "tp", [(i, i ^ d) for i in range(4)]) for d in (1, 2, 3)]

    bounds = (0, cut, rows)
    ends = [jnp.where(z == 1, l2[i:j], r2[i:j]) for i, j in zip(bounds, bounds[1:])]
    ends = lax.optimization_barrier((*ends, *shares))[: len(ends)]
    far = [lax.ppermute(end, "tp", [(1, 0), (2, 3)]) for end in ends]
    acc = add_part(info, 4, [l1, r2, l2], query_weight, acc, shares, up, blocks)
    weight = fetch_part(after(info, acc), 7, query_weight, features.shape[1])
    out = add_part(info, 6, [l2, r2, far[0]], weight, acc, final=(0, cut, None))
    return add_part(info, 6, [l2, r2, far[1]], weight, acc, final=(cut, rows, out))


def anywhere(features, query_weight, adapter_down, adapter_up, block_owner, block_slot, rep):
    asked, source, place = wanted(block_owner, block_slot, rep)
    lists = [swap(asked[i], i, rep) for i in range(1, rep)]
    downs = [swap(p, i + 1, rep) for i, p in enumerate(pack(lists, adapter_down))]
    ups = [swap(p, i + 1, rep) for i, p in enumerate(pack(lists, adapter_up))]
    total = lax.psum(shrink(source, place, features, adapter_down, downs), "tp")
    base = dot(lax.all_gather(features, "tp", axis=1, tiled=True), query_weight)
    up = chosen_blocks(source, place, adapter_up, ups)
    return (base + dot(spread(total, block_slot.shape[0]).T, up)).astype(BF16)


def solution(mesh):
    body = on_line_of_four if mesh.shape["tp"] == 4 else anywhere
    placed = (
        P(("groups", "rep"), "tp"),
        P(None, "tp"),
        P("rep", None, "tp"),
        P("rep", None, "tp"),
        P(("groups", "rep"), None),
        P(("groups", "rep")),
    )
    return jax.shard_map(
        functools.partial(body, rep=mesh.shape["rep"]),
        mesh=mesh,
        in_specs=placed,
        out_specs=P(("groups", "rep"), "tp"),
        check_vma=False,
    )
```

```python
import functools

import jax
import jax.numpy as jnp
from jax import lax
from jax.experimental import pallas as pl
from jax.experimental.pallas import tpu as pltpu
from jax.sharding import PartitionSpec as P

F32 = jnp.float32
BF16 = jnp.bfloat16
PIECE = (3, 4)
ANY = pl.BlockSpec(memory_space=pl.ANY)
VMEM = pl.BlockSpec(memory_space=pltpu.VMEM)


def params(mib):
    return pltpu.CompilerParams(vmem_limit_bytes=mib << 20)


def dot(x, w):
    return jnp.dot(x, w, preferred_element_type=F32)


def wanted(block_owner, block_slot, rep):
    owners = block_owner[:, 0]
    blocks = owners.shape[0]
    cap = 2 * blocks // rep
    order = jnp.arange(blocks)
    earlier = (owners[None, :] == owners[:, None]) & (order[None, :] < order[:, None])
    rank = jnp.sum(earlier, axis=1, dtype=jnp.int32)
    source = jnp.bitwise_xor(owners, lax.axis_index("rep"))
    landing = source * cap + rank
    asked = jnp.sum(
        jnp.where(landing[None, :] == jnp.arange(rep * cap)[:, None], block_slot[None, :], 0), axis=1, dtype=jnp.int32
    ).reshape(rep, cap)
    return asked, source, jnp.where(source == 0, block_slot, rank)


def swap(x, distance, rep):
    return lax.ppermute(x, "rep", [(r, r ^ distance) for r in range(rep)])


def after(x, *earlier):
    return lax.optimization_barrier((x,) + earlier)[0]


def in_turn(parts, rep):
    got = []
    for i, part in enumerate(parts):
        got.append(swap(after(part, *got[-1:]), i + 1, rep))
    return got


def pack_kernel(count, cap, *refs):
    lists, pool, outs, sems = refs[:count], refs[count], refs[count + 1 : -1], refs[-1]
    copies = []
    for i in range(count):
        for j in range(cap):
            copies.append(pltpu.make_async_copy(pool.at[lists[i][j]], outs[i].at[j], sems.at[i, j]))
    for copy in copies:
        copy.start()
    for copy in copies:
        copy.wait()


def pack(lists, pool):
    count, cap = len(lists), lists[0].shape[0]
    shape = jax.ShapeDtypeStruct((cap,) + pool.shape[1:], pool.dtype)
    moved = count * cap * pool.shape[1] * pool.shape[2] * 4
    return pl.pallas_call(
        functools.partial(pack_kernel, count, cap),
        out_shape=[shape] * count,
        in_specs=[pl.BlockSpec(memory_space=pltpu.SMEM)] * count + [ANY],
        out_specs=[ANY] * count,
        scratch_shapes=[pltpu.SemaphoreType.DMA((count, cap))],
        cost_estimate=pl.CostEstimate(flops=0, bytes_accessed=moved, transcendentals=0),
        compiler_params=params(8),
        name="pack_blocks",
    )(*lists, pool)


def choose(source, place, pool, held, chosen, sems):
    blocks, rank = source.shape[0], pool.shape[1]

    def each(act):
        for b in range(blocks):
            for i in range(len(held) + 1):

                @pl.when(source[b] == i)
                def _():
                    block = (pool if i == 0 else held[i - 1]).at[place[b]]
                    act(pltpu.make_async_copy(block, chosen.at[pl.ds(b * rank, rank)], sems.at[b]))

    each(lambda copy: copy.start())
    each(lambda copy: copy.wait())


def choose_kernel(source, place, pool, *refs):
    choose(source, place, pool, refs[:-2], refs[-2], refs[-1])


def chosen_blocks(source, place, pool, held):
    blocks = source.shape[0]
    _, rank, depth = pool.shape
    return pl.pallas_call(
        choose_kernel,
        out_shape=jax.ShapeDtypeStruct((blocks * rank, depth), pool.dtype),
        in_specs=[pl.BlockSpec(memory_space=pltpu.SMEM)] * 2 + [ANY] * (1 + len(held)),
        out_specs=ANY,
        scratch_shapes=[pltpu.SemaphoreType.DMA((blocks,))],
        cost_estimate=pl.CostEstimate(flops=0, bytes_accessed=blocks * rank * depth * 4, transcendentals=0),
        compiler_params=params(8),
        name="choose_blocks",
    )(source, place, pool, *held)


def shrink_kernel(source, place, features, pool, *refs):
    held, part, chosen, sems = refs[:-3], refs[-3], refs[-2], refs[-1]
    blocks, rank, rows = source.shape[0], pool.shape[1], features.shape[0]
    choose(source, place, pool, held, chosen, sems)
    every = lax.dot_general(
        chosen[...], features[...], (((1,), (1,)), ((), ())), preferred_element_type=F32
    ).reshape(blocks, rank, rows)
    batch = lax.broadcasted_iota(jnp.int32, every.shape, 2) // (rows // blocks)
    own = batch == lax.broadcasted_iota(jnp.int32, every.shape, 0)
    part[...] = jnp.sum(jnp.where(own, every, 0.0), axis=0)


def shrink(source, place, features, down, held):
    blocks, rows = source.shape[0], features.shape[0]
    _, rank, depth = down.shape
    return pl.pallas_call(
        shrink_kernel,
        out_shape=jax.ShapeDtypeStruct((rank, rows), F32),
        in_specs=[pl.BlockSpec(memory_space=pltpu.SMEM)] * 2 + [VMEM] + [ANY] * (1 + len(held)),
        out_specs=VMEM,
        scratch_shapes=[pltpu.VMEM((blocks * rank, depth), BF16), pltpu.SemaphoreType.DMA((blocks,))],
        cost_estimate=pl.CostEstimate(flops=2 * blocks * rank * rows * depth, bytes_accessed=rows * depth * 2, transcendentals=0),
        compiler_params=params(16),
        name="shrink",
    )(source, place, features, down, *held)


def spread(total, blocks):
    rank, rows = total.shape
    tall = jnp.concatenate([total] * blocks, axis=0)
    batch = lax.broadcasted_iota(jnp.int32, tall.shape, 1) // (rows // blocks)
    own = batch == lax.broadcasted_iota(jnp.int32, tall.shape, 0) // rank
    return jnp.where(own, tall, 0.0).astype(BF16)


def add_kernel(choices, tail, *refs):
    info, cands = refs[0], refs[1 : 1 + choices]
    rest = list(refs[1 + choices :])
    weight = rest.pop(0)
    acc = rest.pop(0) if tail["acc"] else None
    sums = [rest.pop(0) for _ in range(tail["sums"])]
    up = rest.pop(0) if sums else None
    if tail["kept"]:
        rest.pop(0)
    out, x, sem = rest[:3]
    wide = rest[3] if sums else None
    which = info[tail["which"]]

    def each(act):
        for i, cand in enumerate(cands):

            @pl.when(which == i)
            def _():
                rows = x.shape[0]
                first = 0 if cand.shape[0] == rows else tail["first"]
                act(pltpu.make_async_copy(cand.at[pl.ds(first, rows)], x, sem))

    @pl.when(pl.program_id(0) == 0)
    def _():
        each(lambda copy: copy.start())
        if sums:
            wide[...] = spread(sum(s[...] for s in sums), tail["blocks"])
        each(lambda copy: copy.wait())

    tile = out.shape[1]
    if weight.shape[1] == tile:
        total = dot(x[...], weight[...])
    else:
        total = dot(x[...], weight[:, pl.ds(pl.multiple_of(pl.program_id(0) * tile, tile), tile)])
    if acc is not None:
        total = total + acc[...]
    if sums:
        total = total + lax.dot_general(wide[...], up[...], (((0,), (0,)), ((), ())), preferred_element_type=F32)
    out[...] = total.astype(out.dtype)


def add_part(info, at, cands, weight, acc=None, sums=(), up=None, blocks=0, final=None, tile=512):
    whole, depth = cands[0].shape
    cols = weight.shape[1]
    first, end, kept = final if final else (0, whole, None)
    rows = end - first
    tail = {
        "acc": acc is not None,
        "blocks": blocks,
        "sums": len(sums),
        "kept": kept is not None,
        "which": at,
        "first": first,
    }
    args = [info, *cands, weight]
    specs = [ANY] * len(cands)
    if final:
        specs.append(VMEM)
    else:
        specs.append(pl.BlockSpec((depth, tile), lambda j, info: (info[at + 1], j)))
    block = pl.BlockSpec((rows, tile), lambda j, info: (first // rows, j))
    aliases = {}
    if acc is not None:
        if not final:
            aliases[len(args)] = 0
        args.append(acc)
        specs.append(block)
    scratch = [pltpu.VMEM((rows, depth), BF16), pltpu.SemaphoreType.DMA]
    if blocks:
        args += [*sums, up]
        specs += [pl.BlockSpec(s.shape, lambda j, info: (0, 0)) for s in sums]
        specs.append(pl.BlockSpec((up.shape[0], tile), lambda j, info: (0, j)))
        scratch.append(pltpu.VMEM((up.shape[0], rows), BF16))
    if kept is not None:
        aliases[len(args)] = 0
        args.append(kept)
        specs.append(ANY)
    return pl.pallas_call(
        functools.partial(add_kernel, len(cands), tail),
        out_shape=jax.ShapeDtypeStruct((whole, cols), BF16 if final else F32),
        grid_spec=pltpu.PrefetchScalarGridSpec(
            num_scalar_prefetch=1, grid=(cols // tile,), in_specs=specs, out_specs=block, scratch_shapes=scratch
        ),
        input_output_aliases=aliases,
        cost_estimate=pl.CostEstimate(
            flops=2 * rows * depth * cols, bytes_accessed=2 * depth * cols + 8 * rows * cols, transcendentals=0
        ),
        compiler_params=params(24),
        name="add_part",
    )(*args)


def fetch_kernel(at, info, weight, out, sem):
    depth = out.shape[0]
    copy = pltpu.make_async_copy(weight.at[pl.ds(pl.multiple_of(info[at] * depth, depth), depth)], out, sem)
    copy.start()
    copy.wait()


def fetch_part(info, at, weight, depth):
    return pl.pallas_call(
        functools.partial(fetch_kernel, at),
        out_shape=jax.ShapeDtypeStruct((depth, weight.shape[1]), weight.dtype),
        in_specs=[pl.BlockSpec(memory_space=pltpu.SMEM), ANY],
        out_specs=ANY,
        scratch_shapes=[pltpu.SemaphoreType.DMA],
        cost_estimate=pl.CostEstimate(flops=0, bytes_accessed=4 * depth * weight.shape[1], transcendentals=0),
        compiler_params=params(1),
        name="fetch_part",
    )(info, weight)


CHOICES = (
    (0, 0, 0, 1, 2, 2, 2, 3),
    (0, 1, 1, 0, 0, 2, 0, 3),
    (0, 2, 1, 1, 0, 3, 1, 0),
    (0, 3, 1, 2, 1, 1, 2, 0),
)


def on_line_of_four(features, query_weight, adapter_down, adapter_up, block_owner, block_slot, rep):
    z = lax.axis_index("tp")
    info = lax.dynamic_index_in_dim(jnp.array(CHOICES, jnp.int32), z, 0, keepdims=False)
    right, left = [(0, 1), (1, 2), (2, 3)], [(1, 0), (2, 1), (3, 2)]
    rows, blocks = features.shape[0], block_slot.shape[0]
    cut = rows * PIECE[0] // PIECE[1]

    asked, source, place = wanted(block_owner, block_slot, rep)
    r1, l1 = lax.ppermute(features, "tp", right), lax.ppermute(features, "tp", left)
    lists = [swap(asked[i], i, rep) for i in range(1, rep)]
    downs = in_turn(pack(lists, adapter_down), rep)
    acc = add_part(after(info, *lists), 0, [features], query_weight)
    packed = pack([after(lists[0], acc)] + lists[1:], adapter_up)
    r2, l2 = lax.ppermute(after(r1, acc, packed[0], *downs), "tp", right[1:]), lax.ppermute(after(l1, acc, packed[0], *downs), "tp", left[:-1])
    mine = shrink(after(source, acc, r1, l1), place, features, adapter_down, downs)
    acc = add_part(after(info, mine), 2, [l1, r1], query_weight, acc)
    ups = in_turn([after(packed[0], downs[-1]), *packed[1:]], rep)
    up = chosen_blocks(after(source, acc), place, adapter_up, ups)
    ready = after(mine, acc, ups[-1])
    shares = [mine] + [lax.ppermute(ready, "tp", [(i, i ^ d) for i in range(4)]) for d in (1, 2, 3)]

    bounds = (0, cut, rows)
    ends = [jnp.where(z == 1, l2[i:j], r2[i:j]) for i, j in zip(bounds, bounds[1:])]
    ends[0] = after(ends[0], *shares)
    far = [lax.ppermute(end, "tp", [(1, 0), (2, 3)]) for end in ends]
    acc = add_part(info, 4, [l1, r2, l2], query_weight, acc, shares, up, blocks)
    weight = fetch_part(after(info, acc), 7, query_weight, features.shape[1])
    out = add_part(info, 6, [l2, r2, far[0]], weight, acc, final=(0, cut, None), tile=1024)
    return add_part(info, 6, [l2, r2, far[1]], weight, acc, final=(cut, rows, out), tile=1024)


def anywhere(features, query_weight, adapter_down, adapter_up, block_owner, block_slot, rep):
    asked, source, place = wanted(block_owner, block_slot, rep)
    lists = [swap(asked[i], i, rep) for i in range(1, rep)]
    downs = [swap(p, i + 1, rep) for i, p in enumerate(pack(lists, adapter_down))]
    ups = [swap(p, i + 1, rep) for i, p in enumerate(pack(lists, adapter_up))]
    total = lax.psum(shrink(source, place, features, adapter_down, downs), "tp")
    base = dot(lax.all_gather(features, "tp", axis=1, tiled=True), query_weight)
    up = chosen_blocks(source, place, adapter_up, ups)
    return (base + dot(spread(total, block_slot.shape[0]).T, up)).astype(BF16)


def solution(mesh):
    body = on_line_of_four if mesh.shape["tp"] == 4 else anywhere
    placed = (
        P(("groups", "rep"), "tp"),
        P(None, "tp"),
        P("rep", None, "tp"),
        P("rep", None, "tp"),
        P(("groups", "rep"), None),
        P(("groups", "rep")),
    )
    return jax.shard_map(
        functools.partial(body, rep=mesh.shape["rep"]),
        mesh=mesh,
        in_specs=placed,
        out_specs=P(("groups", "rep"), "tp"),
        check_vma=False,
    )
```

```python
import functools

import jax
import jax.numpy as jnp
from jax import lax
from jax.experimental import pallas as pl
from jax.experimental.pallas import tpu as pltpu
from jax.sharding import PartitionSpec as P

F32 = jnp.float32
BF16 = jnp.bfloat16
PIECE = (3, 4)
ANY = pl.BlockSpec(memory_space=pl.ANY)
VMEM = pl.BlockSpec(memory_space=pltpu.VMEM)


def params(mib):
    return pltpu.CompilerParams(vmem_limit_bytes=mib << 20)


def dot(x, w):
    return jnp.dot(x, w, preferred_element_type=F32)


def wanted(block_owner, block_slot, rep):
    owners = block_owner[:, 0]
    blocks = owners.shape[0]
    cap = 2 * blocks // rep
    order = jnp.arange(blocks)
    earlier = (owners[None, :] == owners[:, None]) & (order[None, :] < order[:, None])
    rank = jnp.sum(earlier, axis=1, dtype=jnp.int32)
    source = jnp.bitwise_xor(owners, lax.axis_index("rep"))
    landing = source * cap + rank
    asked = jnp.sum(
        jnp.where(landing[None, :] == jnp.arange(rep * cap)[:, None], block_slot[None, :], 0), axis=1, dtype=jnp.int32
    ).reshape(rep, cap)
    return asked, source, jnp.where(source == 0, block_slot, rank)


def swap(x, distance, rep):
    return lax.ppermute(x, "rep", [(r, r ^ distance) for r in range(rep)])


def after(x, *earlier):
    return lax.optimization_barrier((x,) + earlier)[0]


def in_turn(parts, rep):
    got = []
    for i, part in enumerate(parts):
        got.append(swap(after(part, *got[-1:]), i + 1, rep))
    return got


def pack_kernel(count, cap, *refs):
    lists, pool, outs, sems = refs[:count], refs[count], refs[count + 1 : -1], refs[-1]
    copies = []
    for i in range(count):
        for j in range(cap):
            copies.append(pltpu.make_async_copy(pool.at[lists[i][j]], outs[i].at[j], sems.at[i, j]))
    for copy in copies:
        copy.start()
    for copy in copies:
        copy.wait()


def pack(lists, pool):
    count, cap = len(lists), lists[0].shape[0]
    shape = jax.ShapeDtypeStruct((cap,) + pool.shape[1:], pool.dtype)
    moved = count * cap * pool.shape[1] * pool.shape[2] * 4
    return pl.pallas_call(
        functools.partial(pack_kernel, count, cap),
        out_shape=[shape] * count,
        in_specs=[pl.BlockSpec(memory_space=pltpu.SMEM)] * count + [ANY],
        out_specs=[ANY] * count,
        scratch_shapes=[pltpu.SemaphoreType.DMA((count, cap))],
        cost_estimate=pl.CostEstimate(flops=0, bytes_accessed=moved, transcendentals=0),
        compiler_params=params(8),
        name="pack_blocks",
    )(*lists, pool)


def choose(source, place, pool, held, chosen, sems):
    blocks, rank = source.shape[0], pool.shape[1]

    def each(act):
        for b in range(blocks):
            for i in range(len(held) + 1):

                @pl.when(source[b] == i)
                def _():
                    block = (pool if i == 0 else held[i - 1]).at[place[b]]
                    act(pltpu.make_async_copy(block, chosen.at[pl.ds(b * rank, rank)], sems.at[b]))

    each(lambda copy: copy.start())
    each(lambda copy: copy.wait())


def choose_kernel(source, place, pool, *refs):
    choose(source, place, pool, refs[:-2], refs[-2], refs[-1])


def chosen_blocks(source, place, pool, held):
    blocks = source.shape[0]
    _, rank, depth = pool.shape
    return pl.pallas_call(
        choose_kernel,
        out_shape=jax.ShapeDtypeStruct((blocks * rank, depth), pool.dtype),
        in_specs=[pl.BlockSpec(memory_space=pltpu.SMEM)] * 2 + [ANY] * (1 + len(held)),
        out_specs=ANY,
        scratch_shapes=[pltpu.SemaphoreType.DMA((blocks,))],
        cost_estimate=pl.CostEstimate(flops=0, bytes_accessed=blocks * rank * depth * 4, transcendentals=0),
        compiler_params=params(8),
        name="choose_blocks",
    )(source, place, pool, *held)


def shrink_kernel(source, place, features, pool, *refs):
    held, part, chosen, sems = refs[:-3], refs[-3], refs[-2], refs[-1]
    blocks, rank, rows = source.shape[0], pool.shape[1], features.shape[0]
    choose(source, place, pool, held, chosen, sems)
    every = lax.dot_general(
        chosen[...], features[...], (((1,), (1,)), ((), ())), preferred_element_type=F32
    ).reshape(blocks, rank, rows)
    batch = lax.broadcasted_iota(jnp.int32, every.shape, 2) // (rows // blocks)
    own = batch == lax.broadcasted_iota(jnp.int32, every.shape, 0)
    part[...] = jnp.sum(jnp.where(own, every, 0.0), axis=0)


def shrink(source, place, features, down, held):
    blocks, rows = source.shape[0], features.shape[0]
    _, rank, depth = down.shape
    return pl.pallas_call(
        shrink_kernel,
        out_shape=jax.ShapeDtypeStruct((rank, rows), F32),
        in_specs=[pl.BlockSpec(memory_space=pltpu.SMEM)] * 2 + [VMEM] + [ANY] * (1 + len(held)),
        out_specs=VMEM,
        scratch_shapes=[pltpu.VMEM((blocks * rank, depth), BF16), pltpu.SemaphoreType.DMA((blocks,))],
        cost_estimate=pl.CostEstimate(flops=2 * blocks * rank * rows * depth, bytes_accessed=rows * depth * 2, transcendentals=0),
        compiler_params=params(16),
        name="shrink",
    )(source, place, features, down, *held)


def spread(total, blocks):
    rank, rows = total.shape
    tall = jnp.concatenate([total] * blocks, axis=0)
    batch = lax.broadcasted_iota(jnp.int32, tall.shape, 1) // (rows // blocks)
    own = batch == lax.broadcasted_iota(jnp.int32, tall.shape, 0) // rank
    return jnp.where(own, tall, 0.0).astype(BF16)


def add_kernel(choices, tail, *refs):
    info, cands = refs[0], refs[1 : 1 + choices]
    rest = list(refs[1 + choices :])
    weight = rest.pop(0)
    acc = rest.pop(0) if tail["acc"] else None
    sums = [rest.pop(0) for _ in range(tail["sums"])]
    up = rest.pop(0) if sums else None
    if tail["kept"]:
        rest.pop(0)
    out, x, sem = rest[:3]
    wide = rest[3] if sums else None
    which = info[tail["which"]]

    def each(act):
        for i, cand in enumerate(cands):

            @pl.when(which == i)
            def _():
                rows = x.shape[0]
                first = 0 if cand.shape[0] == rows else tail["first"]
                act(pltpu.make_async_copy(cand.at[pl.ds(first, rows)], x, sem))

    @pl.when(pl.program_id(0) == 0)
    def _():
        each(lambda copy: copy.start())
        if sums:
            wide[...] = spread(sum(s[...] for s in sums), tail["blocks"])
        each(lambda copy: copy.wait())

    tile = out.shape[1]
    if weight.shape[1] == tile:
        total = dot(x[...], weight[...])
    else:
        total = dot(x[...], weight[:, pl.ds(pl.multiple_of(pl.program_id(0) * tile, tile), tile)])
    if acc is not None:
        total = total + acc[...]
    if sums:
        total = total + lax.dot_general(wide[...], up[...], (((0,), (0,)), ((), ())), preferred_element_type=F32)
    out[...] = total.astype(out.dtype)


def add_part(info, at, cands, weight, acc=None, sums=(), up=None, blocks=0, final=None, tile=512):
    whole, depth = cands[0].shape
    cols = weight.shape[1]
    first, end, kept = final if final else (0, whole, None)
    whole = acc.shape[0] if final else whole
    rows = end - first
    tail = {
        "acc": acc is not None,
        "blocks": blocks,
        "sums": len(sums),
        "kept": kept is not None,
        "which": at,
        "first": first,
    }
    args = [info, *cands, weight]
    specs = [ANY] * len(cands)
    if final:
        specs.append(VMEM)
    else:
        specs.append(pl.BlockSpec((depth, tile), lambda j, info: (info[at + 1], j)))
    block = pl.BlockSpec((rows, tile), lambda j, info: (first // rows, j))
    aliases = {}
    if acc is not None:
        if not final:
            aliases[len(args)] = 0
        args.append(acc)
        specs.append(block)
    scratch = [pltpu.VMEM((rows, depth), BF16), pltpu.SemaphoreType.DMA]
    if blocks:
        args += [*sums, up]
        specs += [pl.BlockSpec(s.shape, lambda j, info: (0, 0)) for s in sums]
        specs.append(pl.BlockSpec((up.shape[0], tile), lambda j, info: (0, j)))
        scratch.append(pltpu.VMEM((up.shape[0], rows), BF16))
    if kept is not None:
        aliases[len(args)] = 0
        args.append(kept)
        specs.append(ANY)
    return pl.pallas_call(
        functools.partial(add_kernel, len(cands), tail),
        out_shape=jax.ShapeDtypeStruct((whole, cols), BF16 if final else F32),
        grid_spec=pltpu.PrefetchScalarGridSpec(
            num_scalar_prefetch=1, grid=(cols // tile,), in_specs=specs, out_specs=block, scratch_shapes=scratch
        ),
        input_output_aliases=aliases,
        cost_estimate=pl.CostEstimate(
            flops=2 * rows * depth * cols, bytes_accessed=2 * depth * cols + 8 * rows * cols, transcendentals=0
        ),
        compiler_params=params(24),
        name="add_part",
    )(*args)


def fetch_kernel(at, info, weight, out, sem):
    depth = out.shape[0]
    copy = pltpu.make_async_copy(weight.at[pl.ds(pl.multiple_of(info[at] * depth, depth), depth)], out, sem)
    copy.start()
    copy.wait()


def fetch_part(info, at, weight, depth):
    return pl.pallas_call(
        functools.partial(fetch_kernel, at),
        out_shape=jax.ShapeDtypeStruct((depth, weight.shape[1]), weight.dtype),
        in_specs=[pl.BlockSpec(memory_space=pltpu.SMEM), ANY],
        out_specs=ANY,
        scratch_shapes=[pltpu.SemaphoreType.DMA],
        cost_estimate=pl.CostEstimate(flops=0, bytes_accessed=4 * depth * weight.shape[1], transcendentals=0),
        compiler_params=params(1),
        name="fetch_part",
    )(info, weight)


CHOICES = (
    (0, 0, 0, 1, 1, 2, 1, 3),
    (0, 1, 1, 0, 0, 2, 0, 3),
    (0, 2, 1, 1, 0, 3, 0, 0),
    (0, 3, 1, 2, 2, 1, 1, 0),
)


def on_line_of_four(features, query_weight, adapter_down, adapter_up, block_owner, block_slot, rep):
    z = lax.axis_index("tp")
    info = lax.dynamic_index_in_dim(jnp.array(CHOICES, jnp.int32), z, 0, keepdims=False)
    right, left = [(0, 1), (1, 2), (2, 3)], [(1, 0), (2, 1), (3, 2)]
    rows, blocks = features.shape[0], block_slot.shape[0]
    cut = rows * PIECE[0] // PIECE[1]

    asked, source, place = wanted(block_owner, block_slot, rep)
    r1, l1 = lax.ppermute(features, "tp", right), lax.ppermute(features, "tp", left)
    lists = [swap(asked[i], i, rep) for i in range(1, rep)]
    downs = [swap(p, i + 1, rep) for i, p in enumerate(pack(lists, adapter_down))]
    acc = add_part(after(info, *lists), 0, [features], query_weight)
    packed = pack([after(lists[0], acc)] + lists[1:], adapter_up)
    mine = shrink(after(source, acc, packed[0]), place, features, adapter_down, downs)
    pair = mine + lax.ppermute(mine, "tp", [(i, i ^ 1) for i in range(4)])

    l2, r2 = lax.ppermute(after(l1, pair), "tp", [(1, 0)]), lax.ppermute(after(r1, pair), "tp", [(2, 3)])
    inner, bounds = after(z, pair), (0, cut, rows)
    cross = [
        lax.ppermute(jnp.where(inner == 1, r1[i:j], l1[i:j]), "tp", [(1, 2), (2, 1)]) for i, j in zip(bounds, bounds[1:])
    ]
    far = [lax.ppermute(c, "tp", [(1, 0), (2, 3)]) for c in cross]

    ups = in_turn([after(packed[0], pair), *packed[1:]], rep)
    shares = [pair, lax.ppermute(after(pair, ups[-1]), "tp", [(i, i ^ 2) for i in range(4)])]
    acc = add_part(after(info, pair), 2, [l1, r1], query_weight, acc)
    up = chosen_blocks(after(source, acc), place, adapter_up, ups)
    acc = add_part(info, 4, [l1, l2, r2], query_weight, acc, shares, up, blocks)
    weight = fetch_part(after(info, acc), 7, query_weight, features.shape[1])
    out = add_part(info, 6, [cross[0], far[0]], weight, acc, final=(0, cut, None), tile=1024)
    return add_part(info, 6, [cross[1], far[1]], weight, acc, final=(cut, rows, out), tile=1024)


def anywhere(features, query_weight, adapter_down, adapter_up, block_owner, block_slot, rep):
    asked, source, place = wanted(block_owner, block_slot, rep)
    lists = [swap(asked[i], i, rep) for i in range(1, rep)]
    downs = [swap(p, i + 1, rep) for i, p in enumerate(pack(lists, adapter_down))]
    ups = [swap(p, i + 1, rep) for i, p in enumerate(pack(lists, adapter_up))]
    total = lax.psum(shrink(source, place, features, adapter_down, downs), "tp")
    base = dot(lax.all_gather(features, "tp", axis=1, tiled=True), query_weight)
    up = chosen_blocks(source, place, adapter_up, ups)
    return (base + dot(spread(total, block_slot.shape[0]).T, up)).astype(BF16)


def solution(mesh):
    body = on_line_of_four if mesh.shape["tp"] == 4 else anywhere
    placed = (
        P(("groups", "rep"), "tp"),
        P(None, "tp"),
        P("rep", None, "tp"),
        P("rep", None, "tp"),
        P(("groups", "rep"), None),
        P(("groups", "rep")),
    )
    return jax.shard_map(
        functools.partial(body, rep=mesh.shape["rep"]),
        mesh=mesh,
        in_specs=placed,
        out_specs=P(("groups", "rep"), "tp"),
        check_vma=False,
    )
```

```python
import functools

import jax
import jax.numpy as jnp
from jax import lax
from jax.experimental import pallas as pl
from jax.experimental.pallas import tpu as pltpu
from jax.sharding import PartitionSpec as P

F32 = jnp.float32
BF16 = jnp.bfloat16
PIECE = (3, 4)
ANY = pl.BlockSpec(memory_space=pl.ANY)
VMEM = pl.BlockSpec(memory_space=pltpu.VMEM)


def params(mib):
    return pltpu.CompilerParams(vmem_limit_bytes=mib << 20)


def dot(x, w):
    return jnp.dot(x, w, preferred_element_type=F32)


def wanted(block_owner, block_slot, rep):
    owners = block_owner[:, 0]
    blocks = owners.shape[0]
    cap = 2 * blocks // rep
    order = jnp.arange(blocks)
    earlier = (owners[None, :] == owners[:, None]) & (order[None, :] < order[:, None])
    rank = jnp.sum(earlier, axis=1, dtype=jnp.int32)
    source = jnp.bitwise_xor(owners, lax.axis_index("rep"))
    landing = source * cap + rank
    asked = jnp.sum(
        jnp.where(landing[None, :] == jnp.arange(rep * cap)[:, None], block_slot[None, :], 0), axis=1, dtype=jnp.int32
    ).reshape(rep, cap)
    return asked, source, jnp.where(source == 0, block_slot, rank)


def swap(x, distance, rep):
    return lax.ppermute(x, "rep", [(r, r ^ distance) for r in range(rep)])


def after(x, *earlier):
    return lax.optimization_barrier((x,) + earlier)[0]


def in_turn(parts, rep):
    got = []
    for i, part in enumerate(parts):
        got.append(swap(after(part, *got[-1:]), i + 1, rep))
    return got


def pack_kernel(count, cap, *refs):
    lists, pool, outs, sems = refs[:count], refs[count], refs[count + 1 : -1], refs[-1]
    copies = []
    for i in range(count):
        for j in range(cap):
            copies.append(pltpu.make_async_copy(pool.at[lists[i][j]], outs[i].at[j], sems.at[i, j]))
    for copy in copies:
        copy.start()
    for copy in copies:
        copy.wait()


def pack(lists, pool):
    count, cap = len(lists), lists[0].shape[0]
    shape = jax.ShapeDtypeStruct((cap,) + pool.shape[1:], pool.dtype)
    moved = count * cap * pool.shape[1] * pool.shape[2] * 4
    return pl.pallas_call(
        functools.partial(pack_kernel, count, cap),
        out_shape=[shape] * count,
        in_specs=[pl.BlockSpec(memory_space=pltpu.SMEM)] * count + [ANY],
        out_specs=[ANY] * count,
        scratch_shapes=[pltpu.SemaphoreType.DMA((count, cap))],
        cost_estimate=pl.CostEstimate(flops=0, bytes_accessed=moved, transcendentals=0),
        compiler_params=params(8),
        name="pack_blocks",
    )(*lists, pool)


def choose(source, place, pool, held, chosen, sems):
    blocks, rank = source.shape[0], pool.shape[1]

    def each(act):
        for b in range(blocks):
            for i in range(len(held) + 1):

                @pl.when(source[b] == i)
                def _():
                    block = (pool if i == 0 else held[i - 1]).at[place[b]]
                    act(pltpu.make_async_copy(block, chosen.at[pl.ds(b * rank, rank)], sems.at[b]))

    each(lambda copy: copy.start())
    each(lambda copy: copy.wait())


def choose_kernel(source, place, pool, *refs):
    choose(source, place, pool, refs[:-2], refs[-2], refs[-1])


def chosen_blocks(source, place, pool, held):
    blocks = source.shape[0]
    _, rank, depth = pool.shape
    return pl.pallas_call(
        choose_kernel,
        out_shape=jax.ShapeDtypeStruct((blocks * rank, depth), pool.dtype),
        in_specs=[pl.BlockSpec(memory_space=pltpu.SMEM)] * 2 + [ANY] * (1 + len(held)),
        out_specs=ANY,
        scratch_shapes=[pltpu.SemaphoreType.DMA((blocks,))],
        cost_estimate=pl.CostEstimate(flops=0, bytes_accessed=blocks * rank * depth * 4, transcendentals=0),
        compiler_params=params(8),
        name="choose_blocks",
    )(source, place, pool, *held)


def shrink_kernel(source, place, features, pool, *refs):
    held, part, chosen, sems = refs[:-3], refs[-3], refs[-2], refs[-1]
    blocks, rank, rows = source.shape[0], pool.shape[1], features.shape[0]
    choose(source, place, pool, held, chosen, sems)
    every = lax.dot_general(
        chosen[...], features[...], (((1,), (1,)), ((), ())), preferred_element_type=F32
    ).reshape(blocks, rank, rows)
    batch = lax.broadcasted_iota(jnp.int32, every.shape, 2) // (rows // blocks)
    own = batch == lax.broadcasted_iota(jnp.int32, every.shape, 0)
    part[...] = jnp.sum(jnp.where(own, every, 0.0), axis=0)


def shrink(source, place, features, down, held):
    blocks, rows = source.shape[0], features.shape[0]
    _, rank, depth = down.shape
    return pl.pallas_call(
        shrink_kernel,
        out_shape=jax.ShapeDtypeStruct((rank, rows), F32),
        in_specs=[pl.BlockSpec(memory_space=pltpu.SMEM)] * 2 + [VMEM] + [ANY] * (1 + len(held)),
        out_specs=VMEM,
        scratch_shapes=[pltpu.VMEM((blocks * rank, depth), BF16), pltpu.SemaphoreType.DMA((blocks,))],
        cost_estimate=pl.CostEstimate(flops=2 * blocks * rank * rows * depth, bytes_accessed=rows * depth * 2, transcendentals=0),
        compiler_params=params(16),
        name="shrink",
    )(source, place, features, down, *held)


def spread(total, blocks):
    rank, rows = total.shape
    tall = jnp.concatenate([total] * blocks, axis=0)
    batch = lax.broadcasted_iota(jnp.int32, tall.shape, 1) // (rows // blocks)
    own = batch == lax.broadcasted_iota(jnp.int32, tall.shape, 0) // rank
    return jnp.where(own, tall, 0.0).astype(BF16)


def add_kernel(tail, *refs):
    info, rest = refs[0], list(refs[1:])
    cands = [[rest.pop(0) for _ in range(n)] for n in tail["cands"]]
    weight = rest.pop(0)
    acc = rest.pop(0) if tail["acc"] else None
    sums = [rest.pop(0) for _ in range(tail["sums"])]
    up = rest.pop(0) if sums else None
    if tail["kept"]:
        rest.pop(0)
    out, x, sems = rest[:3]
    wide = rest[3] if sums else None
    which = info[tail["which"]]

    def each(act):
        for i, cand in enumerate(cands):

            @pl.when(which == i)
            def _():
                first = 0
                for c, piece in enumerate(cand):
                    rows = piece.shape[0]
                    act(pltpu.make_async_copy(piece, x.at[pl.ds(first, rows)], sems.at[c]))
                    first += rows

    @pl.when(pl.program_id(0) == 0)
    def _():
        each(lambda copy: copy.start())
        if sums:
            wide[...] = spread(sum(s[...] for s in sums), tail["blocks"])
        each(lambda copy: copy.wait())

    tile = out.shape[1]
    if weight.shape[1] == tile:
        total = dot(x[...], weight[...])
    else:
        total = dot(x[...], weight[:, pl.ds(pl.multiple_of(pl.program_id(0) * tile, tile), tile)])
    if acc is not None:
        total = total + acc[...]
    if sums:
        total = total + lax.dot_general(wide[...], up[...], (((0,), (0,)), ((), ())), preferred_element_type=F32)
    out[...] = total.astype(out.dtype)


def add_part(info, at, cands, weight, acc=None, sums=(), up=None, blocks=0, final=None, tile=512):
    rows, depth = sum(p.shape[0] for p in cands[0]), cands[0][0].shape[1]
    cols = weight.shape[1]
    first, kept = final if final else (0, None)
    tail = {
        "cands": [len(c) for c in cands],
        "acc": acc is not None,
        "blocks": blocks,
        "sums": len(sums),
        "kept": kept is not None,
        "which": at,
    }
    args = [info] + [p for cand in cands for p in cand] + [weight]
    specs = [ANY] * (len(args) - 2)
    if final:
        specs.append(VMEM)
    else:
        specs.append(pl.BlockSpec((depth, tile), lambda j, info: (info[at + 1], j)))
    block = pl.BlockSpec((rows, tile), lambda j, info: (first // rows, j))
    aliases = {}
    if acc is not None:
        if not final:
            aliases[len(args)] = 0
        args.append(acc)
        specs.append(block)
    most = max(tail["cands"])
    scratch = [pltpu.VMEM((rows, depth), BF16), pltpu.SemaphoreType.DMA((most,))]
    if sums:
        args += [*sums, up]
        specs += [pl.BlockSpec(s.shape, lambda j, info: (0, 0)) for s in sums]
        specs.append(pl.BlockSpec((up.shape[0], tile), lambda j, info: (0, j)))
        scratch.append(pltpu.VMEM((up.shape[0], rows), BF16))
    if kept is not None:
        aliases[len(args)] = 0
        args.append(kept)
        specs.append(ANY)
    return pl.pallas_call(
        functools.partial(add_kernel, tail),
        out_shape=jax.ShapeDtypeStruct((acc.shape[0] if final else rows, cols), BF16 if final else F32),
        grid_spec=pltpu.PrefetchScalarGridSpec(
            num_scalar_prefetch=1, grid=(cols // tile,), in_specs=specs, out_specs=block, scratch_shapes=scratch
        ),
        input_output_aliases=aliases,
        cost_estimate=pl.CostEstimate(
            flops=2 * rows * depth * cols, bytes_accessed=2 * depth * cols + 8 * rows * cols, transcendentals=0
        ),
        compiler_params=params(24),
        name="add_part",
    )(*args)


def split_kernel(starts, count, *refs):
    arrays, outs, sems = refs[:count], refs[count:-1], refs[-1]
    copies = []
    for c, (first, end) in enumerate(zip(starts, starts[1:])):
        for k, x in enumerate(arrays):
            at = c * count + k
            copies.append(pltpu.make_async_copy(x.at[pl.ds(first, end - first)], outs[at], sems.at[at]))
    for copy in copies:
        copy.start()
    for copy in copies:
        copy.wait()


def split_rows(arrays, starts):
    shapes = [jax.ShapeDtypeStruct((b - a, x.shape[1]), x.dtype) for a, b in zip(starts, starts[1:]) for x in arrays]
    return pl.pallas_call(
        functools.partial(split_kernel, starts, len(arrays)),
        out_shape=shapes,
        in_specs=[ANY] * len(arrays),
        out_specs=[ANY] * len(shapes),
        scratch_shapes=[pltpu.SemaphoreType.DMA((len(shapes),))],
        cost_estimate=pl.CostEstimate(flops=0, bytes_accessed=sum(4 * x.size for x in arrays), transcendentals=0),
        compiler_params=params(1),
        name="split_rows",
    )(*arrays)


def fetch_kernel(at, info, weight, out, sem):
    depth = out.shape[0]
    copy = pltpu.make_async_copy(weight.at[pl.ds(pl.multiple_of(info[at] * depth, depth), depth)], out, sem)
    copy.start()
    copy.wait()


def fetch_part(info, at, weight, depth):
    return pl.pallas_call(
        functools.partial(fetch_kernel, at),
        out_shape=jax.ShapeDtypeStruct((depth, weight.shape[1]), weight.dtype),
        in_specs=[pl.BlockSpec(memory_space=pltpu.SMEM), ANY],
        out_specs=ANY,
        scratch_shapes=[pltpu.SemaphoreType.DMA],
        cost_estimate=pl.CostEstimate(flops=0, bytes_accessed=4 * depth * weight.shape[1], transcendentals=0),
        compiler_params=params(1),
        name="fetch_part",
    )(info, weight)


CHOICES = (
    (0, 0, 0, 1, 1, 2, 1, 3),
    (0, 1, 0, 0, 0, 2, 0, 3),
    (0, 2, 0, 3, 0, 1, 0, 0),
    (0, 3, 0, 2, 1, 1, 1, 0),
)


def on_line_of_four(features, query_weight, adapter_down, adapter_up, block_owner, block_slot, rep):
    z = lax.axis_index("tp")
    info = lax.dynamic_index_in_dim(jnp.array(CHOICES, jnp.int32), z, 0, keepdims=False)
    outer, middle, outward = [(i, i ^ 1) for i in range(4)], [(1, 2), (2, 1)], [(1, 0), (2, 3)]
    rows, blocks = features.shape[0], block_slot.shape[0]
    cut = rows * PIECE[0] // PIECE[1]

    asked, source, place = wanted(block_owner, block_slot, rep)
    near = lax.ppermute(features, "tp", outer)
    across = lax.ppermute(features, "tp", middle)
    lists = [swap(asked[i], i, rep) for i in range(1, rep)]
    downs = [swap(p, i + 1, rep) for i, p in enumerate(pack(lists, adapter_down))]
    acc = add_part(after(info, *lists), 0, [[features]], query_weight)
    packed = pack([after(lists[0], acc)] + lists[1:], adapter_up)
    mine = shrink(after(source, acc, packed[0]), place, features, adapter_down, downs)
    pair = mine + lax.ppermute(mine, "tp", outer)
    shares = [pair, lax.ppermute(pair, "tp", [(i, i ^ 2) for i in range(4)])]
    held = after(near, *shares[:1])
    halves = held[:cut], held[cut:]
    passed = lax.ppermute(after(across, *shares[:1]), "tp", outward)
    inner = [lax.ppermute(p, "tp", middle) for p in halves]
    last = [lax.ppermute(p, "tp", outward) for p in inner]

    ups = in_turn([after(packed[0], *shares[:1]), *packed[1:]], rep)
    acc = add_part(after(info, *shares[:1]), 2, [[near]], query_weight, acc)
    base = acc
    up = chosen_blocks(after(source, acc), place, adapter_up, ups)
    acc = add_part(info, 4, [[across], [passed]], query_weight, acc, shares, up, blocks)
    weight = fetch_part(after(info, base), 7, query_weight, features.shape[1])
    out = add_part(info, 6, [inner[:1], last[:1]], weight, acc, final=(0, None), tile=1024)
    return add_part(info, 6, [inner[1:], last[1:]], weight, acc, final=(cut, out), tile=1024)


def anywhere(features, query_weight, adapter_down, adapter_up, block_owner, block_slot, rep):
    asked, source, place = wanted(block_owner, block_slot, rep)
    lists = [swap(asked[i], i, rep) for i in range(1, rep)]
    downs = [swap(p, i + 1, rep) for i, p in enumerate(pack(lists, adapter_down))]
    ups = [swap(p, i + 1, rep) for i, p in enumerate(pack(lists, adapter_up))]
    total = lax.psum(shrink(source, place, features, adapter_down, downs), "tp")
    base = dot(lax.all_gather(features, "tp", axis=1, tiled=True), query_weight)
    up = chosen_blocks(source, place, adapter_up, ups)
    return (base + dot(spread(total, block_slot.shape[0]).T, up)).astype(BF16)


def solution(mesh):
    body = on_line_of_four if mesh.shape["tp"] == 4 else anywhere
    placed = (
        P(("groups", "rep"), "tp"),
        P(None, "tp"),
        P("rep", None, "tp"),
        P("rep", None, "tp"),
        P(("groups", "rep"), None),
        P(("groups", "rep")),
    )
    return jax.shard_map(
        functools.partial(body, rep=mesh.shape["rep"]),
        mesh=mesh,
        in_specs=placed,
        out_specs=P(("groups", "rep"), "tp"),
        check_vma=False,
    )
```

```python
import functools

import jax
import jax.numpy as jnp
from jax import lax
from jax.experimental import pallas as pl
from jax.experimental.pallas import tpu as pltpu
from jax.sharding import PartitionSpec as P

F32 = jnp.float32
BF16 = jnp.bfloat16
PIECE = (3, 4)
ANY = pl.BlockSpec(memory_space=pl.ANY)
VMEM = pl.BlockSpec(memory_space=pltpu.VMEM)


def params(mib):
    return pltpu.CompilerParams(vmem_limit_bytes=mib << 20)


def dot(x, w):
    return jnp.dot(x, w, preferred_element_type=F32)


def wanted(block_owner, block_slot, rep):
    owners = block_owner[:, 0]
    blocks = owners.shape[0]
    cap = 2 * blocks // rep
    order = jnp.arange(blocks)
    earlier = (owners[None, :] == owners[:, None]) & (order[None, :] < order[:, None])
    rank = jnp.sum(earlier, axis=1, dtype=jnp.int32)
    source = jnp.bitwise_xor(owners, lax.axis_index("rep"))
    landing = source * cap + rank
    asked = jnp.sum(
        jnp.where(landing[None, :] == jnp.arange(rep * cap)[:, None], block_slot[None, :], 0), axis=1, dtype=jnp.int32
    ).reshape(rep, cap)
    return asked, source, jnp.where(source == 0, block_slot, rank)


def swap(x, distance, rep):
    return lax.ppermute(x, "rep", [(r, r ^ distance) for r in range(rep)])


def after(x, *earlier):
    return lax.optimization_barrier((x,) + earlier)[0]


def in_turn(parts, rep):
    got = []
    for i, part in enumerate(parts):
        got.append(swap(after(part, *got[-1:]), i + 1, rep))
    return got


def pack_kernel(count, cap, *refs):
    lists, pool, outs, sems = refs[:count], refs[count], refs[count + 1 : -1], refs[-1]
    copies = []
    for i in range(count):
        for j in range(cap):
            copies.append(pltpu.make_async_copy(pool.at[lists[i][j]], outs[i].at[j], sems.at[i, j]))
    for copy in copies:
        copy.start()
    for copy in copies:
        copy.wait()


def pack(lists, pool):
    count, cap = len(lists), lists[0].shape[0]
    shape = jax.ShapeDtypeStruct((cap,) + pool.shape[1:], pool.dtype)
    moved = count * cap * pool.shape[1] * pool.shape[2] * 4
    return pl.pallas_call(
        functools.partial(pack_kernel, count, cap),
        out_shape=[shape] * count,
        in_specs=[pl.BlockSpec(memory_space=pltpu.SMEM)] * count + [ANY],
        out_specs=[ANY] * count,
        scratch_shapes=[pltpu.SemaphoreType.DMA((count, cap))],
        cost_estimate=pl.CostEstimate(flops=0, bytes_accessed=moved, transcendentals=0),
        compiler_params=params(8),
        name="pack_blocks",
    )(*lists, pool)


def choose(source, place, pool, held, chosen, sems):
    blocks, rank = source.shape[0], pool.shape[1]

    def each(act):
        for b in range(blocks):
            for i in range(len(held) + 1):

                @pl.when(source[b] == i)
                def _():
                    block = (pool if i == 0 else held[i - 1]).at[place[b]]
                    act(pltpu.make_async_copy(block, chosen.at[pl.ds(b * rank, rank)], sems.at[b]))

    each(lambda copy: copy.start())
    each(lambda copy: copy.wait())


def choose_kernel(source, place, pool, *refs):
    choose(source, place, pool, refs[:-2], refs[-2], refs[-1])


def chosen_blocks(source, place, pool, held):
    blocks = source.shape[0]
    _, rank, depth = pool.shape
    return pl.pallas_call(
        choose_kernel,
        out_shape=jax.ShapeDtypeStruct((blocks * rank, depth), pool.dtype),
        in_specs=[pl.BlockSpec(memory_space=pltpu.SMEM)] * 2 + [ANY] * (1 + len(held)),
        out_specs=ANY,
        scratch_shapes=[pltpu.SemaphoreType.DMA((blocks,))],
        cost_estimate=pl.CostEstimate(flops=0, bytes_accessed=blocks * rank * depth * 4, transcendentals=0),
        compiler_params=params(8),
        name="choose_blocks",
    )(source, place, pool, *held)


def shrink_kernel(source, place, features, pool, *refs):
    held, part, chosen, sems = refs[:-3], refs[-3], refs[-2], refs[-1]
    blocks, rank, rows = source.shape[0], pool.shape[1], features.shape[0]
    choose(source, place, pool, held, chosen, sems)
    every = lax.dot_general(
        chosen[...], features[...], (((1,), (1,)), ((), ())), preferred_element_type=F32
    ).reshape(blocks, rank, rows)
    batch = lax.broadcasted_iota(jnp.int32, every.shape, 2) // (rows // blocks)
    own = batch == lax.broadcasted_iota(jnp.int32, every.shape, 0)
    part[...] = jnp.sum(jnp.where(own, every, 0.0), axis=0)


def shrink(source, place, features, down, held):
    blocks, rows = source.shape[0], features.shape[0]
    _, rank, depth = down.shape
    return pl.pallas_call(
        shrink_kernel,
        out_shape=jax.ShapeDtypeStruct((rank, rows), F32),
        in_specs=[pl.BlockSpec(memory_space=pltpu.SMEM)] * 2 + [VMEM] + [ANY] * (1 + len(held)),
        out_specs=VMEM,
        scratch_shapes=[pltpu.VMEM((blocks * rank, depth), BF16), pltpu.SemaphoreType.DMA((blocks,))],
        cost_estimate=pl.CostEstimate(flops=2 * blocks * rank * rows * depth, bytes_accessed=rows * depth * 2, transcendentals=0),
        compiler_params=params(16),
        name="shrink",
    )(source, place, features, down, *held)


def spread(total, blocks):
    rank, rows = total.shape
    tall = jnp.concatenate([total] * blocks, axis=0)
    batch = lax.broadcasted_iota(jnp.int32, tall.shape, 1) // (rows // blocks)
    own = batch == lax.broadcasted_iota(jnp.int32, tall.shape, 0) // rank
    return jnp.where(own, tall, 0.0).astype(BF16)


def add_kernel(tail, *refs):
    info, rest = refs[0], list(refs[1:])
    cands = [[rest.pop(0) for _ in range(n)] for n in tail["cands"]]
    weight = rest.pop(0)
    acc = rest.pop(0) if tail["acc"] else None
    sums = [rest.pop(0) for _ in range(tail["sums"])]
    up = rest.pop(0) if sums else None
    if tail["kept"]:
        rest.pop(0)
    out, x, sems = rest[:3]
    wide = rest[3] if sums else None
    which = info[tail["which"]]

    def each(act):
        for i, cand in enumerate(cands):

            @pl.when(which == i)
            def _():
                first = 0
                for c, piece in enumerate(cand):
                    rows = piece.shape[0]
                    act(pltpu.make_async_copy(piece, x.at[pl.ds(first, rows)], sems.at[c]))
                    first += rows

    @pl.when(pl.program_id(0) == 0)
    def _():
        each(lambda copy: copy.start())
        if sums:
            wide[...] = spread(sum(s[...] for s in sums), tail["blocks"])
        each(lambda copy: copy.wait())

    tile = out.shape[1]
    if weight.shape[1] == tile:
        total = dot(x[...], weight[...])
    else:
        total = dot(x[...], weight[:, pl.ds(pl.multiple_of(pl.program_id(0) * tile, tile), tile)])
    if acc is not None:
        total = total + acc[...]
    if sums:
        total = total + lax.dot_general(wide[...], up[...], (((0,), (0,)), ((), ())), preferred_element_type=F32)
    out[...] = total.astype(out.dtype)


def add_part(info, at, cands, weight, acc=None, sums=(), up=None, blocks=0, final=None, tile=512):
    rows, depth = sum(p.shape[0] for p in cands[0]), cands[0][0].shape[1]
    cols = weight.shape[1]
    first, kept = final if final else (0, None)
    tail = {
        "cands": [len(c) for c in cands],
        "acc": acc is not None,
        "blocks": blocks,
        "sums": len(sums),
        "kept": kept is not None,
        "which": at,
    }
    args = [info] + [p for cand in cands for p in cand] + [weight]
    specs = [ANY] * (len(args) - 2)
    if final:
        specs.append(VMEM)
    else:
        specs.append(pl.BlockSpec((depth, tile), lambda j, info: (info[at + 1], j)))
    block = pl.BlockSpec((rows, tile), lambda j, info: (first // rows, j))
    aliases = {}
    if acc is not None:
        if not final:
            aliases[len(args)] = 0
        args.append(acc)
        specs.append(block)
    most = max(tail["cands"])
    scratch = [pltpu.VMEM((rows, depth), BF16), pltpu.SemaphoreType.DMA((most,))]
    if sums:
        args += [*sums, up]
        specs += [pl.BlockSpec(s.shape, lambda j, info: (0, 0)) for s in sums]
        specs.append(pl.BlockSpec((up.shape[0], tile), lambda j, info: (0, j)))
        scratch.append(pltpu.VMEM((up.shape[0], rows), BF16))
    if kept is not None:
        aliases[len(args)] = 0
        args.append(kept)
        specs.append(ANY)
    return pl.pallas_call(
        functools.partial(add_kernel, tail),
        out_shape=jax.ShapeDtypeStruct((acc.shape[0] if final else rows, cols), BF16 if final else F32),
        grid_spec=pltpu.PrefetchScalarGridSpec(
            num_scalar_prefetch=1, grid=(cols // tile,), in_specs=specs, out_specs=block, scratch_shapes=scratch
        ),
        input_output_aliases=aliases,
        cost_estimate=pl.CostEstimate(
            flops=2 * rows * depth * cols, bytes_accessed=2 * depth * cols + 8 * rows * cols, transcendentals=0
        ),
        compiler_params=params(24),
        name="add_part",
    )(*args)


def split_kernel(starts, count, *refs):
    arrays, outs, sems = refs[:count], refs[count:-1], refs[-1]
    copies = []
    for c, (first, end) in enumerate(zip(starts, starts[1:])):
        for k, x in enumerate(arrays):
            at = c * count + k
            copies.append(pltpu.make_async_copy(x.at[pl.ds(first, end - first)], outs[at], sems.at[at]))
    for copy in copies:
        copy.start()
    for copy in copies:
        copy.wait()


def split_rows(arrays, starts):
    shapes = [jax.ShapeDtypeStruct((b - a, x.shape[1]), x.dtype) for a, b in zip(starts, starts[1:]) for x in arrays]
    return pl.pallas_call(
        functools.partial(split_kernel, starts, len(arrays)),
        out_shape=shapes,
        in_specs=[ANY] * len(arrays),
        out_specs=[ANY] * len(shapes),
        scratch_shapes=[pltpu.SemaphoreType.DMA((len(shapes),))],
        cost_estimate=pl.CostEstimate(flops=0, bytes_accessed=sum(4 * x.size for x in arrays), transcendentals=0),
        compiler_params=params(1),
        name="split_rows",
    )(*arrays)


def fetch_kernel(at, info, weight, out, sem):
    depth = out.shape[0]
    copy = pltpu.make_async_copy(weight.at[pl.ds(pl.multiple_of(info[at] * depth, depth), depth)], out, sem)
    copy.start()
    copy.wait()


def fetch_part(info, at, weight, depth):
    return pl.pallas_call(
        functools.partial(fetch_kernel, at),
        out_shape=jax.ShapeDtypeStruct((depth, weight.shape[1]), weight.dtype),
        in_specs=[pl.BlockSpec(memory_space=pltpu.SMEM), ANY],
        out_specs=ANY,
        scratch_shapes=[pltpu.SemaphoreType.DMA],
        cost_estimate=pl.CostEstimate(flops=0, bytes_accessed=4 * depth * weight.shape[1], transcendentals=0),
        compiler_params=params(1),
        name="fetch_part",
    )(info, weight)


CHOICES = (
    (0, 0, 0, 1, 1, 2, 1, 3),
    (0, 1, 0, 0, 0, 2, 0, 3),
    (0, 2, 0, 3, 0, 1, 0, 0),
    (0, 3, 0, 2, 1, 1, 1, 0),
)


def on_line_of_four(features, query_weight, adapter_down, adapter_up, block_owner, block_slot, rep):
    z = lax.axis_index("tp")
    info = lax.dynamic_index_in_dim(jnp.array(CHOICES, jnp.int32), z, 0, keepdims=False)
    outer, middle, outward = [(i, i ^ 1) for i in range(4)], [(1, 2), (2, 1)], [(1, 0), (2, 3)]
    rows, blocks = features.shape[0], block_slot.shape[0]
    cut = rows * PIECE[0] // PIECE[1]

    asked, source, place = wanted(block_owner, block_slot, rep)
    near = lax.ppermute(features, "tp", outer)
    across = lax.ppermute(features, "tp", middle)
    lists = [swap(asked[i], i, rep) for i in range(1, rep)]
    downs = [swap(p, i + 1, rep) for i, p in enumerate(pack(lists, adapter_down))]
    acc = add_part(after(info, *lists), 0, [[features]], query_weight)
    packed = pack([after(lists[0], acc)] + lists[1:], adapter_up)
    mine = shrink(after(source, acc, packed[0]), place, features, adapter_down, downs)
    pair = mine + lax.ppermute(mine, "tp", outer)
    shares = [pair, lax.ppermute(pair, "tp", [(i, i ^ 2) for i in range(4)])]
    held = after(near, *shares[:1])
    halves = held[:cut], held[cut:]
    passed = lax.ppermute(after(across, *shares[:1]), "tp", outward)
    inner = [lax.ppermute(p, "tp", middle) for p in halves]
    ups = in_turn([after(packed[0], *shares[:1]), *packed[1:]], rep)
    acc = add_part(after(info, *shares[:1]), 2, [[near]], query_weight, acc)
    base = acc
    last = [lax.ppermute(p, "tp", outward) for p in (after(inner[0], acc), inner[1])]
    up = chosen_blocks(after(source, acc), place, adapter_up, ups)
    acc = add_part(info, 4, [[across], [passed]], query_weight, acc, shares, up, blocks)
    weight = fetch_part(after(info, base), 7, query_weight, features.shape[1])
    out = add_part(info, 6, [inner[:1], last[:1]], weight, acc, final=(0, None), tile=1024)
    return add_part(info, 6, [inner[1:], last[1:]], weight, acc, final=(cut, out), tile=1024)


def anywhere(features, query_weight, adapter_down, adapter_up, block_owner, block_slot, rep):
    asked, source, place = wanted(block_owner, block_slot, rep)
    lists = [swap(asked[i], i, rep) for i in range(1, rep)]
    downs = [swap(p, i + 1, rep) for i, p in enumerate(pack(lists, adapter_down))]
    ups = [swap(p, i + 1, rep) for i, p in enumerate(pack(lists, adapter_up))]
    total = lax.psum(shrink(source, place, features, adapter_down, downs), "tp")
    base = dot(lax.all_gather(features, "tp", axis=1, tiled=True), query_weight)
    up = chosen_blocks(source, place, adapter_up, ups)
    return (base + dot(spread(total, block_slot.shape[0]).T, up)).astype(BF16)


def solution(mesh):
    body = on_line_of_four if mesh.shape["tp"] == 4 else anywhere
    placed = (
        P(("groups", "rep"), "tp"),
        P(None, "tp"),
        P("rep", None, "tp"),
        P("rep", None, "tp"),
        P(("groups", "rep"), None),
        P(("groups", "rep")),
    )
    return jax.shard_map(
        functools.partial(body, rep=mesh.shape["rep"]),
        mesh=mesh,
        in_specs=placed,
        out_specs=P(("groups", "rep"), "tp"),
        check_vma=False,
    )
```

```python
import functools

import jax
import jax.numpy as jnp
from jax import lax
from jax.experimental import pallas as pl
from jax.experimental.pallas import tpu as pltpu
from jax.sharding import PartitionSpec as P

F32 = jnp.float32
BF16 = jnp.bfloat16
PIECE = (3, 4)
ANY = pl.BlockSpec(memory_space=pl.ANY)
VMEM = pl.BlockSpec(memory_space=pltpu.VMEM)


def params(mib):
    return pltpu.CompilerParams(vmem_limit_bytes=mib << 20)


def dot(x, w):
    return jnp.dot(x, w, preferred_element_type=F32)


def wanted(block_owner, block_slot, rep):
    owners = block_owner[:, 0]
    blocks = owners.shape[0]
    cap = 2 * blocks // rep
    order = jnp.arange(blocks)
    earlier = (owners[None, :] == owners[:, None]) & (order[None, :] < order[:, None])
    rank = jnp.sum(earlier, axis=1, dtype=jnp.int32)
    source = jnp.bitwise_xor(owners, lax.axis_index("rep"))
    landing = source * cap + rank
    asked = jnp.sum(
        jnp.where(landing[None, :] == jnp.arange(rep * cap)[:, None], block_slot[None, :], 0), axis=1, dtype=jnp.int32
    ).reshape(rep, cap)
    return asked, source, jnp.where(source == 0, block_slot, rank)


def swap(x, distance, rep):
    return lax.ppermute(x, "rep", [(r, r ^ distance) for r in range(rep)])


def after(x, *earlier):
    return lax.optimization_barrier((x,) + earlier)[0]


def in_turn(parts, rep):
    got = []
    for i, part in enumerate(parts):
        got.append(swap(after(part, *got[-1:]), i + 1, rep))
    return got


def pack_kernel(count, cap, *refs):
    lists, pool, outs, sems = refs[:count], refs[count], refs[count + 1 : -1], refs[-1]
    copies = []
    for i in range(count):
        for j in range(cap):
            copies.append(pltpu.make_async_copy(pool.at[lists[i][j]], outs[i].at[j], sems.at[i, j]))
    for copy in copies:
        copy.start()
    for copy in copies:
        copy.wait()


def pack(lists, pool):
    count, cap = len(lists), lists[0].shape[0]
    shape = jax.ShapeDtypeStruct((cap,) + pool.shape[1:], pool.dtype)
    moved = count * cap * pool.shape[1] * pool.shape[2] * 4
    return pl.pallas_call(
        functools.partial(pack_kernel, count, cap),
        out_shape=[shape] * count,
        in_specs=[pl.BlockSpec(memory_space=pltpu.SMEM)] * count + [ANY],
        out_specs=[ANY] * count,
        scratch_shapes=[pltpu.SemaphoreType.DMA((count, cap))],
        cost_estimate=pl.CostEstimate(flops=0, bytes_accessed=moved, transcendentals=0),
        compiler_params=params(8),
        name="pack_blocks",
    )(*lists, pool)


def choose(source, place, pool, held, chosen, sems):
    blocks, rank = source.shape[0], pool.shape[1]

    def each(act):
        for b in range(blocks):
            for i in range(len(held) + 1):

                @pl.when(source[b] == i)
                def _():
                    block = (pool if i == 0 else held[i - 1]).at[place[b]]
                    act(pltpu.make_async_copy(block, chosen.at[pl.ds(b * rank, rank)], sems.at[b]))

    each(lambda copy: copy.start())
    each(lambda copy: copy.wait())


def choose_kernel(source, place, pool, *refs):
    choose(source, place, pool, refs[:-2], refs[-2], refs[-1])


def chosen_blocks(source, place, pool, held):
    blocks = source.shape[0]
    _, rank, depth = pool.shape
    return pl.pallas_call(
        choose_kernel,
        out_shape=jax.ShapeDtypeStruct((blocks * rank, depth), pool.dtype),
        in_specs=[pl.BlockSpec(memory_space=pltpu.SMEM)] * 2 + [ANY] * (1 + len(held)),
        out_specs=ANY,
        scratch_shapes=[pltpu.SemaphoreType.DMA((blocks,))],
        cost_estimate=pl.CostEstimate(flops=0, bytes_accessed=blocks * rank * depth * 4, transcendentals=0),
        compiler_params=params(8),
        name="choose_blocks",
    )(source, place, pool, *held)


def shrink_kernel(source, place, features, pool, *refs):
    held, part, chosen, sems = refs[:-3], refs[-3], refs[-2], refs[-1]
    blocks, rank, rows = source.shape[0], pool.shape[1], features.shape[0]
    choose(source, place, pool, held, chosen, sems)
    every = lax.dot_general(
        chosen[...], features[...], (((1,), (1,)), ((), ())), preferred_element_type=F32
    ).reshape(blocks, rank, rows)
    batch = lax.broadcasted_iota(jnp.int32, every.shape, 2) // (rows // blocks)
    own = batch == lax.broadcasted_iota(jnp.int32, every.shape, 0)
    part[...] = jnp.sum(jnp.where(own, every, 0.0), axis=0)


def shrink(source, place, features, down, held):
    blocks, rows = source.shape[0], features.shape[0]
    _, rank, depth = down.shape
    return pl.pallas_call(
        shrink_kernel,
        out_shape=jax.ShapeDtypeStruct((rank, rows), F32),
        in_specs=[pl.BlockSpec(memory_space=pltpu.SMEM)] * 2 + [VMEM] + [ANY] * (1 + len(held)),
        out_specs=VMEM,
        scratch_shapes=[pltpu.VMEM((blocks * rank, depth), BF16), pltpu.SemaphoreType.DMA((blocks,))],
        cost_estimate=pl.CostEstimate(flops=2 * blocks * rank * rows * depth, bytes_accessed=rows * depth * 2, transcendentals=0),
        compiler_params=params(16),
        name="shrink",
    )(source, place, features, down, *held)


def spread(total, blocks):
    rank, rows = total.shape
    tall = jnp.concatenate([total] * blocks, axis=0)
    batch = lax.broadcasted_iota(jnp.int32, tall.shape, 1) // (rows // blocks)
    own = batch == lax.broadcasted_iota(jnp.int32, tall.shape, 0) // rank
    return jnp.where(own, tall, 0.0).astype(BF16)


def add_kernel(tail, *refs):
    info, rest = refs[0], list(refs[1:])
    cands = [[rest.pop(0) for _ in range(n)] for n in tail["cands"]]
    weight = rest.pop(0)
    acc = rest.pop(0) if tail["acc"] else None
    sums = [rest.pop(0) for _ in range(tail["sums"])]
    up = rest.pop(0) if sums else None
    if tail["kept"]:
        rest.pop(0)
    out, x, sems = rest[:3]
    wide = rest[3] if sums else None
    which = info[tail["which"]]

    def each(act):
        for i, cand in enumerate(cands):

            @pl.when(which == i)
            def _():
                first = 0
                for c, piece in enumerate(cand):
                    rows = piece.shape[0]
                    act(pltpu.make_async_copy(piece, x.at[pl.ds(first, rows)], sems.at[c]))
                    first += rows

    @pl.when(pl.program_id(0) == 0)
    def _():
        each(lambda copy: copy.start())
        if sums:
            wide[...] = spread(sum(s[...] for s in sums), tail["blocks"])
        each(lambda copy: copy.wait())

    tile = out.shape[1]
    if weight.shape[1] == tile:
        total = dot(x[...], weight[...])
    else:
        total = dot(x[...], weight[:, pl.ds(pl.multiple_of(pl.program_id(0) * tile, tile), tile)])
    if acc is not None:
        total = total + acc[...]
    if sums:
        total = total + lax.dot_general(wide[...], up[...], (((0,), (0,)), ((), ())), preferred_element_type=F32)
    out[...] = total.astype(out.dtype)


def add_part(info, at, cands, weight, acc=None, sums=(), up=None, blocks=0, final=None, tile=512):
    rows, depth = sum(p.shape[0] for p in cands[0]), cands[0][0].shape[1]
    cols = weight.shape[1]
    first, kept = final if final else (0, None)
    tail = {
        "cands": [len(c) for c in cands],
        "acc": acc is not None,
        "blocks": blocks,
        "sums": len(sums),
        "kept": kept is not None,
        "which": at,
    }
    args = [info] + [p for cand in cands for p in cand] + [weight]
    specs = [ANY] * (len(args) - 2)
    if final:
        specs.append(VMEM)
    else:
        specs.append(pl.BlockSpec((depth, tile), lambda j, info: (info[at + 1], j)))
    block = pl.BlockSpec((rows, tile), lambda j, info: (first // rows, j))
    aliases = {}
    if acc is not None:
        if not final:
            aliases[len(args)] = 0
        args.append(acc)
        specs.append(block)
    most = max(tail["cands"])
    scratch = [pltpu.VMEM((rows, depth), BF16), pltpu.SemaphoreType.DMA((most,))]
    if sums:
        args += [*sums, up]
        specs += [pl.BlockSpec(s.shape, lambda j, info: (0, 0)) for s in sums]
        specs.append(pl.BlockSpec((up.shape[0], tile), lambda j, info: (0, j)))
        scratch.append(pltpu.VMEM((up.shape[0], rows), BF16))
    if kept is not None:
        aliases[len(args)] = 0
        args.append(kept)
        specs.append(ANY)
    return pl.pallas_call(
        functools.partial(add_kernel, tail),
        out_shape=jax.ShapeDtypeStruct((acc.shape[0] if final else rows, cols), BF16 if final else F32),
        grid_spec=pltpu.PrefetchScalarGridSpec(
            num_scalar_prefetch=1, grid=(cols // tile,), in_specs=specs, out_specs=block, scratch_shapes=scratch
        ),
        input_output_aliases=aliases,
        cost_estimate=pl.CostEstimate(
            flops=2 * rows * depth * cols, bytes_accessed=2 * depth * cols + 8 * rows * cols, transcendentals=0
        ),
        compiler_params=params(24),
        name="add_part",
    )(*args)


def split_kernel(starts, count, *refs):
    arrays, outs, sems = refs[:count], refs[count:-1], refs[-1]
    copies = []
    for c, (first, end) in enumerate(zip(starts, starts[1:])):
        for k, x in enumerate(arrays):
            at = c * count + k
            copies.append(pltpu.make_async_copy(x.at[pl.ds(first, end - first)], outs[at], sems.at[at]))
    for copy in copies:
        copy.start()
    for copy in copies:
        copy.wait()


def split_rows(arrays, starts):
    shapes = [jax.ShapeDtypeStruct((b - a, x.shape[1]), x.dtype) for a, b in zip(starts, starts[1:]) for x in arrays]
    return pl.pallas_call(
        functools.partial(split_kernel, starts, len(arrays)),
        out_shape=shapes,
        in_specs=[ANY] * len(arrays),
        out_specs=[ANY] * len(shapes),
        scratch_shapes=[pltpu.SemaphoreType.DMA((len(shapes),))],
        cost_estimate=pl.CostEstimate(flops=0, bytes_accessed=sum(4 * x.size for x in arrays), transcendentals=0),
        compiler_params=params(1),
        name="split_rows",
    )(*arrays)


def fetch_kernel(at, info, weight, out, sem):
    depth = out.shape[0]
    copy = pltpu.make_async_copy(weight.at[pl.ds(pl.multiple_of(info[at] * depth, depth), depth)], out, sem)
    copy.start()
    copy.wait()


def fetch_part(info, at, weight, depth):
    return pl.pallas_call(
        functools.partial(fetch_kernel, at),
        out_shape=jax.ShapeDtypeStruct((depth, weight.shape[1]), weight.dtype),
        in_specs=[pl.BlockSpec(memory_space=pltpu.SMEM), ANY],
        out_specs=ANY,
        scratch_shapes=[pltpu.SemaphoreType.DMA],
        cost_estimate=pl.CostEstimate(flops=0, bytes_accessed=4 * depth * weight.shape[1], transcendentals=0),
        compiler_params=params(1),
        name="fetch_part",
    )(info, weight)


CHOICES = (
    (0, 0, 0, 1, 1, 2, 1, 3),
    (0, 1, 0, 0, 0, 2, 0, 3),
    (0, 2, 0, 3, 0, 1, 0, 0),
    (0, 3, 0, 2, 1, 1, 1, 0),
)


def on_line_of_four(features, query_weight, adapter_down, adapter_up, block_owner, block_slot, rep):
    z = lax.axis_index("tp")
    info = lax.dynamic_index_in_dim(jnp.array(CHOICES, jnp.int32), z, 0, keepdims=False)
    outer, middle, outward = [(i, i ^ 1) for i in range(4)], [(1, 2), (2, 1)], [(1, 0), (2, 3)]
    rows, blocks = features.shape[0], block_slot.shape[0]
    cut = rows * PIECE[0] // PIECE[1]

    asked, source, place = wanted(block_owner, block_slot, rep)
    near = lax.ppermute(features, "tp", outer)
    across = lax.ppermute(features, "tp", middle)
    lists = [swap(asked[i], i, rep) for i in range(1, rep)]
    downs = [swap(p, i + 1, rep) for i, p in enumerate(pack(lists, adapter_down))]
    acc = add_part(after(info, *lists), 0, [[features]], query_weight)
    packed = pack([after(lists[0], acc)] + lists[1:], adapter_up)
    mine = shrink(after(source, acc, packed[0]), place, features, adapter_down, downs)
    pair = mine + lax.ppermute(mine, "tp", outer)
    shares = [pair, lax.ppermute(pair, "tp", [(i, i ^ 2) for i in range(4)])]
    held = after(near, *shares[:1])
    halves = held[:cut], held[cut:]
    passed = lax.ppermute(after(across, *shares[:1]), "tp", outward)
    inner = [lax.ppermute(p, "tp", middle) for p in halves]
    ups = in_turn([after(packed[0], *shares[:1]), *packed[1:]], rep)
    acc = add_part(after(info, *shares[:1]), 2, [[near]], query_weight, acc)
    weight = fetch_part(after(info, acc), 7, query_weight, features.shape[1])
    last = [lax.ppermute(p, "tp", outward) for p in (after(inner[0], weight), inner[1])]
    up = chosen_blocks(after(source, acc), place, adapter_up, ups)
    acc = add_part(info, 4, [[across], [passed]], query_weight, acc, shares, up, blocks)
    out = add_part(info, 6, [inner[:1], last[:1]], weight, acc, final=(0, None), tile=2048)
    return add_part(info, 6, [inner[1:], last[1:]], weight, acc, final=(cut, out), tile=2048)


def anywhere(features, query_weight, adapter_down, adapter_up, block_owner, block_slot, rep):
    asked, source, place = wanted(block_owner, block_slot, rep)
    lists = [swap(asked[i], i, rep) for i in range(1, rep)]
    downs = [swap(p, i + 1, rep) for i, p in enumerate(pack(lists, adapter_down))]
    ups = [swap(p, i + 1, rep) for i, p in enumerate(pack(lists, adapter_up))]
    total = lax.psum(shrink(source, place, features, adapter_down, downs), "tp")
    base = dot(lax.all_gather(features, "tp", axis=1, tiled=True), query_weight)
    up = chosen_blocks(source, place, adapter_up, ups)
    return (base + dot(spread(total, block_slot.shape[0]).T, up)).astype(BF16)


def solution(mesh):
    body = on_line_of_four if mesh.shape["tp"] == 4 else anywhere
    placed = (
        P(("groups", "rep"), "tp"),
        P(None, "tp"),
        P("rep", None, "tp"),
        P("rep", None, "tp"),
        P(("groups", "rep"), None),
        P(("groups", "rep")),
    )
    return jax.shard_map(
        functools.partial(body, rep=mesh.shape["rep"]),
        mesh=mesh,
        in_specs=placed,
        out_specs=P(("groups", "rep"), "tp"),
        check_vma=False,
    )
```
